512 devices in a mesh: dp: 32 (over z_lo, y, core), ctx: 16 (over z_hi, x).
Axes of the slice: x: 4, y: 8, z: 8 (z_hi: 4, z_lo: 2; z = z_hi * 2 + z_lo), core: 2. Of those that a mesh axis runs over, the one named last changes fastest.
Arguments:
- tokens: bfloat16 [32, 4096, 3072], P('dp', 'ctx'), may hold values from -6 to 6
- queries: bfloat16 [32, 4096, 2048], P('dp', 'ctx'), may hold values from -6 to 6
- master: float32 [3072, 2048], P(('dp', 'ctx')), may hold values from -0.5051815 to 0.5051815
- grad: float32 [3072, 2048], P(('dp', 'ctx')), may hold values from -6 to 6
- moment: float32 [3072, 2048], P(('dp', 'ctx')), may hold values from -4 to 4
- second: float32 [3072, 2048], P(('dp', 'ctx')), may hold values from 0.05 to 4
Outputs:
- new_master: float32 [3072, 2048], P(('dp', 'ctx'))
- new_moment: float32 [3072, 2048], P(('dp', 'ctx'))
- new_second: float32 [3072, 2048], P(('dp', 'ctx'))
- codes: bfloat16 [3072, 2048], P(('dp', 'ctx'))
- attended: bfloat16 [32, 4096, 2048], P('dp', 'ctx')
The draws below stay inside these ranges and needn't reach their ends.
All inputs are finite; a program needn't handle non-finite values. Where the reference program divides by a largest or mean magnitude, that divisor is 1e-20 or more.
Results may differ from the reference program's by a relative error of at most 0.0091.
Values may be sent and summed in bfloat16 or wider, within the bound.
A program may use at most 128 MiB of HBM per device.

```python
import math
import jax
import jax.numpy as jnp
from jax import lax

D = 3072
HD = 128
KVH = 8
WINDOW = 512
TOK_DEV = 256
GROUP = 2
KVW = 2048
QW = 2048
SEQ = 4096
BATCH = 32
N_CTX = 16


def draw_master(key, part):
    key = jax.random.fold_in(key, 11)
    first, middle, last = jax.random.split(key, 3)
    row_scale = jnp.exp(jax.random.uniform(first, (D, 1), jnp.float32) * math.log(10.0))
    col_scale = jnp.exp(jax.random.uniform(middle, (1, KVW), jnp.float32) * math.log(10.0))
    base = jnp.clip(jax.random.normal(last, (D, KVW), jnp.float32), -6.0, 6.0)
    return base * row_scale * col_scale * (0.0465 / math.sqrt(D))


def shard_levels(stream_key, extent, cuts, low, top_value):
    loudness = 1.0
    for axis_at, blocks in cuts:
        draws = jax.random.uniform(jax.random.fold_in(jax.random.fold_in(stream_key, 6), axis_at), (blocks,), jnp.float32, low / len(cuts), top_value / len(cuts))
        loudness = loudness * jnp.repeat(jnp.exp(draws), extent[axis_at] // blocks).reshape((-1,) + (1,) * (len(extent) - 1 - axis_at))
    return loudness


def scatter_about(own_key, extent, scale, limit, cuts=(), kind=jnp.bfloat16):
    drawn = jax.random.normal(own_key, extent, jnp.float32) * scale
    if len(cuts) > 0:
        drawn = shard_levels(own_key, extent, cuts, -0.22, 0.18) * drawn
    return jnp.clip(drawn, min=-limit, max=limit).astype(kind)


def setup_inputs(seed: int = 0) -> dict:
    key_list = jax.random.split(jax.random.key(seed), 7)
    return {
        "tokens": scatter_about(key_list[0], (BATCH, SEQ, D), 1.0, 6.0, ((0, 32), (1, 16))),
        "queries": scatter_about(key_list[1], (BATCH, SEQ, QW), 1.0, 6.0, ((0, 32), (1, 16))),
        "master": draw_master(jax.random.fold_in(key_list[6], 71), 0),
        "grad": scatter_about(key_list[3], (D, KVW), 1.0, 6.0, ((0, 512),), jnp.float32),
        "moment": scatter_about(key_list[4], (D, KVW), 0.3, 4.0, ((0, 512),), jnp.float32),
        "second": jnp.clip(jnp.exp(math.log(4.0) - 4.3820266 * jax.random.uniform(key_list[5], (D, KVW), jnp.float32) ** shard_levels(key_list[5], (D, KVW), ((0, 512),), -0.2, 0.2)), 0.05, 4.0),
    }


beta_one = 0.9
beta_two = 0.95
adam_eps = 1e-08
decay_rate = 0.1
learn_rate = 0.001
step_count = 1000
score_scale = 1.0 / 12.0
soft_cap = 50.0
rope_base = 10000.0

def adamw(master, grad, moment, second):
    new_moment = beta_one * moment + (1.0 - beta_one) * grad
    new_second = beta_two * second + (1.0 - beta_two) * grad * grad
    moment_hat = new_moment / (1.0 - beta_one ** step_count)
    second_hat = new_second / (1.0 - beta_two ** step_count)
    update = moment_hat / (jnp.sqrt(second_hat) + adam_eps) + decay_rate * master
    return (master - learn_rate * update, new_moment, new_second)

def rotate_keys(product, peak, positions):
    scaled = product * peak[None, :]
    half = HD // 2
    keys = scaled[:, :KVH * HD].reshape(-1, KVH, HD)
    values = scaled[:, KVH * HD:]
    freqs = rope_base ** (-jnp.arange(half, dtype=jnp.float32) * 2.0 / HD)
    angles = positions.astype(jnp.float32)[:, None] * freqs[None, :]
    cosine = jnp.cos(angles)[:, None, :]
    sine = jnp.sin(angles)[:, None, :]
    lower = keys[..., :half]
    upper = keys[..., half:]
    turned = jnp.concatenate([lower * cosine - upper * sine, upper * cosine + lower * sine], axis=-1)
    turned = turned.reshape(-1, KVH * HD)
    return jnp.concatenate([turned, values], axis=1).astype(jnp.bfloat16)

def attend(query_rows, key_rows, query_start, key_start):
    rows = query_rows.shape[0]
    span = key_rows.shape[0]
    qpos = query_start + jnp.arange(rows, dtype=jnp.int32)
    kpos = key_start + jnp.arange(span, dtype=jnp.int32)
    gap = qpos[:, None] - kpos[None, :]
    valid = (gap >= 0) & (gap < WINDOW) & (kpos[None, :] >= 0)
    grouped = query_rows.reshape(rows, KVH, GROUP * HD).transpose(1, 0, 2)
    keys = key_rows[:, :KVH * HD].reshape(span, KVH, HD).transpose(1, 0, 2)
    values = key_rows[:, KVH * HD:].reshape(span, KVH, HD).transpose(1, 0, 2)

    def one_head(triple):
        query_head, key_head, value_head = triple
        query_head = query_head.reshape(rows, GROUP, HD).astype(jnp.float32)
        scores = jnp.einsum('rgd,sd->grs', query_head, key_head.astype(jnp.float32)) * score_scale
        capped = soft_cap * jnp.tanh(scores / soft_cap)
        weights = jnp.where(valid[None], jnp.exp(capped), jnp.zeros_like(capped))
        probs = (weights / lax.optimization_barrier(jnp.sum(weights, axis=-1, keepdims=True))).astype(jnp.bfloat16)
        mixed = jnp.einsum('grs,sd->rgd', probs.astype(jnp.float32), value_head.astype(jnp.float32))
        return mixed.astype(jnp.bfloat16)
    heads = lax.map(one_head, (grouped, keys, values))
    return heads.transpose(1, 0, 2, 3).reshape(rows, KVH * GROUP * HD)

def reference(tokens, queries, master, grad, moment, second):
    new_master, new_moment, new_second = adamw(master, grad, moment, second)
    peak = lax.optimization_barrier(jnp.max(jnp.abs(new_master), axis=0)) + 1e-06
    codes = (new_master / peak[None, :]).astype(jnp.bfloat16)

    def one_sequence(pair):
        rows, query_rows = pair
        product = jnp.dot(rows, codes, preferred_element_type=jnp.float32)
        keyval = rotate_keys(product, peak, jnp.arange(SEQ, dtype=jnp.int32))
        padded = jnp.concatenate([jnp.zeros((WINDOW, KVW), jnp.bfloat16), keyval], axis=0)

        def block(index):
            start = (index * TOK_DEV).astype(jnp.int32)
            key_rows = lax.dynamic_slice_in_dim(padded, start, WINDOW + TOK_DEV, 0)
            block_queries = lax.dynamic_slice_in_dim(query_rows, start, TOK_DEV, 0)
            return attend(block_queries, key_rows, start, start - WINDOW)
        return lax.map(block, jnp.arange(N_CTX, dtype=jnp.int32)).reshape(SEQ, QW)
    attended = lax.map(one_sequence, (tokens, queries))
    return (new_master, new_moment, new_second, codes, attended)
```

```python
import functools

import jax
import jax.numpy as jnp
from jax import lax
from jax.experimental import pallas as pl
from jax.experimental.pallas import tpu as pltpu
from jax.sharding import PartitionSpec as P

HD = 128
KVH = 8
WINDOW = 512
GROUP = 2
ROWS = 256
WIDTH = 3072
KVW = 2048

beta_one = 0.9
beta_two = 0.95
adam_eps = 1e-08
decay_rate = 0.1
learn_rate = 0.001
step_count = 1000
soft_cap = 50.0
rope_base = 10000.0

MESH = pl.DeviceIdType.MESH
HEADS = 4
LOG2E = 1.4426950408889634


def rem(a, b):
    return lax.rem(a, jnp.int32(b))


def div(a, b):
    return lax.div(a, jnp.int32(b))


def kernel(
    tok_hbm, q_hbm, master, grad, moment, second, cosine, sine,
    attended, new_master, new_moment, new_second, codes,
    weights, tok, qs, keyval, sent_out, staged, pieces, block, peaks,
    tok_sem, q_sem, piece_sem, x_send, x_recv, first_send, first_recv,
    ring_send, ring_recv, halo_send, halo_recv, out_send, out_recv, peak_sem,
):
    dp, ctx = lax.axis_index("dp"), lax.axis_index("ctx")
    core, y, z_lo = rem(dp, 2), rem(div(dp, 2), 8), div(dp, 16)
    x, z_hi = rem(ctx, 4), div(ctx, 4)
    z = 2 * z_hi + z_lo
    kind, half = div(z_hi, 2), rem(z_hi, 2)
    row_group = (z_lo * 8 + y) * 2

    def device(xx, yy, zz):
        return ((rem(zz, 2) * 8 + yy) * 2 + core, div(zz, 2) * 4 + xx)

    sibling = (row_group + 1 - core, ctx)
    barrier = pltpu.get_barrier_semaphore()

    def greet(i, _):
        to_core, to_ctx = rem(i, 2), div(i, 2)

        @pl.when((to_core != core) | (to_ctx != ctx))
        def _():
            pl.semaphore_signal(
                barrier, inc=1, device_id=(row_group + to_core, to_ctx), device_id_type=MESH
            )

        return 0

    lax.fori_loop(0, 32, greet, 0)

    def greet_y(k, _):
        pl.semaphore_signal(
            barrier, inc=1, device_id=device(x, rem(y + k, 8), z), device_id_type=MESH
        )
        return 0

    lax.fori_loop(1, 8, greet_y, 0)

    def greet_z(k, _):
        pl.semaphore_signal(
            barrier, inc=1, device_id=device(x, y, rem(z + 2 * k + 1, 8)), device_id_type=MESH
        )
        return 0

    lax.fori_loop(0, 4, greet_z, 0)

    own_cols = pl.ds(pl.multiple_of(core * 1024, 1024), 1024)
    their_cols = pl.ds(pl.multiple_of((1 - core) * 1024, 1024), 1024)
    own_tok = pltpu.make_async_copy(tok_hbm, tok.at[0], tok_sem.at[0])
    own_q = pltpu.make_async_copy(q_hbm.at[:, own_cols], qs.at[0], q_sem.at[0])
    own_tok.start()
    own_q.start()

    g = grad[...]
    old = master[...]
    mom = beta_one * moment[...] + (1.0 - beta_one) * g
    sec = beta_two * second[...] + (1.0 - beta_two) * g * g
    mom_hat = mom / (1.0 - beta_one**step_count)
    sec_hat = sec / (1.0 - beta_two**step_count)
    update = mom_hat / (jnp.sqrt(sec_hat) + adam_eps) + decay_rate * old
    fresh = old - learn_rate * update
    new_master[...] = fresh
    new_moment[...] = mom
    new_second[...] = sec
    staged[...] = jnp.zeros_like(staged)
    for b in range(16):
        staged[b, 0:6, :] = fresh[:, 128 * b : 128 * b + 128]

    pl.semaphore_wait(barrier, 42)

    def owner(b):
        head = rem(b, 8)
        return div(head, 4), (div(b, 8) * 2 + core) * 4 + rem(head, 4)

    def send_piece(b, _):
        to_core, to_ctx = owner(b)
        mine = (to_core == core) & (to_ctx == ctx)

        @pl.when(mine)
        def _():
            pltpu.make_async_copy(staged.at[b], pieces.at[ctx], piece_sem.at[1]).start()

        @pl.when(jnp.logical_not(mine))
        def _():
            pltpu.make_async_remote_copy(
                src_ref=staged.at[b],
                dst_ref=pieces.at[ctx],
                send_sem=piece_sem.at[0],
                recv_sem=piece_sem.at[1],
                device_id=(row_group + to_core, to_ctx),
                device_id_type=MESH,
            ).start()

        return 0

    lax.fori_loop(0, 16, send_piece, 0)
    pltpu.make_async_copy(pieces, pieces, piece_sem.at[1]).wait()

    for j in range(16):
        block[6 * j : 6 * j + 6, :] = pieces[j, 0:6, :]
    weights[x, kind, z_lo, y, half] = block[...].astype(jnp.bfloat16)

    def x_copy(k):
        ref = weights.at[x, kind, z_lo, y, half]
        return pltpu.make_async_remote_copy(
            src_ref=ref, dst_ref=ref, send_sem=x_send.at[k], recv_sem=x_recv.at[k],
            device_id=device(rem(x + k + 1, 4), y, z), device_id_type=MESH,
        )

    for k in range(3):
        x_copy(k).start()

    their_tok = pltpu.make_async_remote_copy(
        src_ref=tok_hbm, dst_ref=tok.at[1], send_sem=tok_sem.at[1], recv_sem=tok_sem.at[2],
        device_id=sibling, device_id_type=MESH,
    )
    their_q = pltpu.make_async_remote_copy(
        src_ref=q_hbm.at[:, their_cols], dst_ref=qs.at[1], send_sem=q_sem.at[1],
        recv_sem=q_sem.at[2], device_id=sibling, device_id_type=MESH,
    )
    their_tok.start()
    their_q.start()

    for k in range(3):
        ref = weights.at[rem(x + 3 - k, 4), kind, z_lo, y, half]
        pltpu.make_async_copy(ref, ref, x_recv.at[k]).wait()

    def first(h, _):
        upper = weights.at[h, kind, z_lo, y, half, pl.ds(0, 48), :]
        lower = weights.at[h, kind, z_lo, y, half, pl.ds(48, 48), :]

        def to_peer(k, _):
            pltpu.make_async_remote_copy(
                src_ref=upper, dst_ref=upper, send_sem=first_send.at[0, h],
                recv_sem=first_recv.at[0, h],
                device_id=device(x, rem(y + k, 8), z), device_id_type=MESH,
            ).start()
            pltpu.make_async_remote_copy(
                src_ref=lower, dst_ref=lower, send_sem=first_send.at[1, h],
                recv_sem=first_recv.at[1, h],
                device_id=device(x, y, rem(z + k, 8)), device_id_type=MESH,
            ).start()
            return 0

        lax.fori_loop(1, 8, to_peer, 0)
        return 0

    lax.fori_loop(0, HEADS, first, 0)

    def wait_first(sems, h):
        for axis in range(2):
            ref = weights.at[h, 0, 0, pl.ds(0, 7), 0, pl.ds(0, 48), :]
            pltpu.make_async_copy(ref, ref, sems.at[axis, h]).wait()

    def part(axis, h, at, which):
        if axis == 0:
            rows = (pl.ds(0, 8), pl.ds(0, 4), pl.ds(4, 4))[which]
            return weights.at[
                h, div(at, 4), rem(at, 2), rows, rem(div(at, 2), 2), pl.ds(0, 48), :
            ]
        kinds = (pl.ds(0, 2), pl.ds(0, 1), pl.ds(1, 1))[which]
        return weights.at[h, kinds, :, at, :, pl.ds(48, 48), :]

    def ring_copy(axis, way, h, step, received):
        here = (z, y)[axis]
        sign = 1 - 2 * way
        origin = rem(here - sign * (step + (1 if received else 0)) + 16, 8)
        which = 0 if step < 3 else 1 + way
        target = rem(here + sign + 8, 8)
        ref = part(axis, h, origin, which)
        return pltpu.make_async_remote_copy(
            src_ref=ref, dst_ref=ref, send_sem=ring_send.at[axis, way, h, step],
            recv_sem=ring_recv.at[axis, way, h, step],
            device_id=device(x, y, target) if axis == 0 else device(x, target, z),
            device_id_type=MESH,
        )

    def ring_start(h, step):
        for axis in range(2):
            for way in range(2):
                ring_copy(axis, way, h, step, False).start()

    def ring_wait(h, step):
        for axis in range(2):
            for way in range(2):
                ring_copy(axis, way, h, step, True).wait_recv()

    def project(h):
        total = jnp.zeros((2 * ROWS, 2 * HD), jnp.float32)
        top = jnp.zeros((8, 2 * HD), jnp.float32)
        for c in range(4):
            low = weights[h, 0, c // 2, 4 * (c % 2) : 4 * (c % 2) + 4].reshape(768, HD)
            high = weights[h, 1, c // 2, 4 * (c % 2) : 4 * (c % 2) + 4].reshape(768, HD)
            both = jnp.concatenate([low, high], axis=1)
            rows = tok[:, :, 768 * c : 768 * c + 768].reshape(2 * ROWS, 768)
            total = total + jnp.dot(rows, both, preferred_element_type=jnp.float32)
            size = jnp.abs(both.astype(jnp.float32)).reshape(96, 8, 2 * HD)
            top = jnp.maximum(top, jnp.max(size, axis=0))
        top = jnp.broadcast_to(jnp.max(top, axis=0, keepdims=True), (8, 2 * HD))
        peaks[core, h, 0] = top[:, :HD]
        peaks[core, h, 1] = top[:, HD:]
        keys = total[:, :HD]
        turned = pltpu.roll(keys, 64, 1)
        for s in range(2):
            span = slice(ROWS * s, ROWS * s + ROWS)
            rotated = keys[span] * cosine[...] + turned[span] * sine[...]
            keyval[h, s, 0, 512:768, :] = rotated.astype(jnp.bfloat16)
            keyval[h, s, 1, 512:768, :] = total[span, HD:].astype(jnp.bfloat16)

    next_ctx = (dp, rem(ctx + 1, 16))

    def halo_copy(h, hop):
        src = keyval.at[h, :, :, pl.ds(512 - 256 * hop, 256), :]
        dst = keyval.at[h, :, :, pl.ds(256 - 256 * hop, 256), :]
        return pltpu.make_async_remote_copy(
            src_ref=src, dst_ref=dst, send_sem=halo_send.at[hop, h],
            recv_sem=halo_recv.at[hop, h], device_id=next_ctx, device_id_type=MESH,
        )

    row_id = lax.broadcasted_iota(jnp.int32, (2 * 128, 128), 0)
    row_id = jnp.where(row_id >= 128, row_id - 128, row_id)
    col_id = lax.broadcasted_iota(jnp.int32, (2 * 128, 128), 1)
    past = col_id > row_id

    def attend(h):
        def one(i, _):
            s, a = div(i, 2), rem(i, 2)
            start = pl.multiple_of(a * 128, 128)
            cols = pl.ds(pl.multiple_of(h * 256, 256), 256)
            q = qs[s, pl.ds(start, 128), cols]
            q = jnp.concatenate([q[:, :HD], q[:, HD:]], axis=0)
            keys = keyval[h, s, 0, pl.ds(start, 640), :]
            values = keyval[h, s, 1, pl.ds(start, 640), :]
            scores = lax.dot_general(
                q, keys, (((1,), (1,)), ((), ())), preferred_element_type=jnp.float32
            )
            weight = jnp.exp2(jnp.tanh(scores * (1.0 / 600.0)) * (soft_cap * LOG2E))
            tiles = []
            for t in range(5):
                tile = weight[:, 128 * t : 128 * t + 128]
                inside = (128 * t - 512 + ctx * 256 + start) >= 0
                if t == 0:
                    tile = jnp.where(past & inside, tile, 0.0)
                elif t == 4:
                    tile = jnp.where(past, 0.0, tile)
                else:
                    tile = jnp.where(inside, tile, 0.0)
                tiles.append(tile)
            norm = jnp.sum(tiles[0] + tiles[1] + tiles[2] + tiles[3] + tiles[4], axis=1, keepdims=True)
            weight = jnp.concatenate([t.astype(jnp.bfloat16) for t in tiles], axis=1)
            mixed = jnp.dot(weight, values, preferred_element_type=jnp.float32)
            mixed = (mixed / norm).astype(jnp.bfloat16)
            mixed = jnp.concatenate([mixed[:128], mixed[128:]], axis=1)

            @pl.when(s == 0)
            def _():
                out_cols = pl.ds(pl.multiple_of(core * 1024 + h * 256, 256), 256)
                attended[pl.ds(start, 128), out_cols] = mixed

            @pl.when(s == 1)
            def _():
                sent_out[h, pl.ds(start, 128), :] = mixed

            return 0

        lax.fori_loop(0, 4, one, 0)

    def out_copy(h):
        out_cols = pl.ds(pl.multiple_of(core * 1024 + h * 256, 256), 256)
        return pltpu.make_async_remote_copy(
            src_ref=sent_out.at[h], dst_ref=attended.at[:, out_cols],
            send_sem=out_send.at[h], recv_sem=out_recv.at[h],
            device_id=sibling, device_id_type=MESH,
        )

    own_tok.wait()
    own_q.wait()
    their_tok.wait()
    their_q.wait()

    def turn(t, _):
        @pl.when(t < 4)
        def _():
            wait_first(first_recv, t)
            ring_start(t, 0)

        @pl.when((t >= 1) & (t < 5))
        def _():
            ring_wait(t - 1, 1)
            ring_start(t - 1, 2)

        @pl.when((t >= 2) & (t < 6))
        def _():
            ring_wait(t - 2, 3)
            project(t - 2)
            halo_copy(t - 2, 0).start()

        @pl.when(t < 4)
        def _():
            ring_wait(t, 0)
            ring_start(t, 1)

        @pl.when((t >= 1) & (t < 5))
        def _():
            ring_wait(t - 1, 2)
            ring_start(t - 1, 3)

        @pl.when((t >= 3) & (t < 7))
        def _():
            halo_copy(t - 3, 0).wait_recv()
            halo_copy(t - 3, 1).start()

        @pl.when(t >= 4)
        def _():
            halo_copy(t - 4, 1).wait_recv()
            attend(t - 4)
            out_copy(t - 4).start()

        return 0

    lax.fori_loop(0, 8, turn, 0)

    peak_copy = pltpu.make_async_remote_copy(
        src_ref=peaks.at[core], dst_ref=peaks.at[core], send_sem=peak_sem.at[0],
        recv_sem=peak_sem.at[1], device_id=sibling, device_id_type=MESH,
    )
    peak_copy.start()

    @pl.when(half == core)
    def _():
        ref = staged.at[pl.ds(0, 15)]
        pltpu.make_async_copy(ref, ref, piece_sem.at[0]).wait()

    @pl.when(half != core)
    def _():
        pltpu.make_async_copy(staged, staged, piece_sem.at[0]).wait()

    for k in range(3):
        x_copy(k).wait_send()

    def drain(h, _):
        wait_first(first_send, h)
        for step in range(4):
            for axis in range(2):
                for way in range(2):
                    ring_copy(axis, way, h, step, False).wait_send()
        halo_copy(h, 0).wait_send()
        halo_copy(h, 1).wait_send()
        out_copy(h).wait_send()
        theirs = pl.ds(pl.multiple_of((1 - core) * 1024 + h * 256, 256), 256)
        ref = attended.at[:, theirs]
        pltpu.make_async_copy(ref, ref, out_recv.at[h]).wait()
        return 0

    lax.fori_loop(0, HEADS, drain, 0)

    peak_copy.wait_send()
    ref = peaks.at[1 - core]
    pltpu.make_async_copy(ref, ref, peak_sem.at[1]).wait()
    for b in range(16):
        head = b % 8
        peak = peaks[head // 4, head % 4, b // 8, 0:1, :] + 1e-06
        codes[:, 128 * b : 128 * b + 128] = (staged[b, 0:6, :] / peak).astype(jnp.bfloat16)


def on_device(tokens, queries, master, grad, moment, second):
    query_start = lax.axis_index("ctx") * ROWS
    positions = query_start + jnp.arange(ROWS, dtype=jnp.int32)
    freqs = rope_base ** (-jnp.arange(HD // 2, dtype=jnp.float32) * 2.0 / HD)
    angles = positions.astype(jnp.float32)[:, None] * freqs[None, :]
    cosine, sine = jnp.cos(angles), jnp.sin(angles)
    cosine = jnp.concatenate([cosine, cosine], axis=1)
    sine = jnp.concatenate([-sine, sine], axis=1)
    vmem = pl.BlockSpec(memory_space=pltpu.VMEM)
    hbm = pl.BlockSpec(memory_space=pl.ANY)
    dma = pltpu.SemaphoreType.DMA
    f32, bf16 = jnp.float32, jnp.bfloat16
    attended, new_master, new_moment, new_second, codes = pl.pallas_call(
        kernel,
        out_shape=(
            jax.ShapeDtypeStruct((ROWS, KVW), bf16),
            jax.ShapeDtypeStruct((6, KVW), f32),
            jax.ShapeDtypeStruct((6, KVW), f32),
            jax.ShapeDtypeStruct((6, KVW), f32),
            jax.ShapeDtypeStruct((6, KVW), bf16),
        ),
        in_specs=[hbm, hbm] + [vmem] * 6,
        out_specs=(vmem,) * 5,
        scratch_shapes=[
            pltpu.VMEM((HEADS, 2, 2, 8, 2, 96, HD), bf16),
            pltpu.VMEM((2, ROWS, WIDTH), bf16),
            pltpu.VMEM((2, ROWS, 1024), bf16),
            pltpu.VMEM((HEADS, 2, 2, 768, HD), bf16),
            pltpu.VMEM((HEADS, ROWS, 256), bf16),
            pltpu.VMEM((16, 8, 128), f32),
            pltpu.VMEM((16, 8, 128), f32),
            pltpu.VMEM((96, 128), f32),
            pltpu.VMEM((2, HEADS, 2, 8, 128), f32),
            dma((3,)),
            dma((3,)),
            dma((2,)),
            dma((3,)),
            dma((3,)),
            dma((2, HEADS)),
            dma((2, HEADS)),
            dma((2, 2, HEADS, 4)),
            dma((2, 2, HEADS, 4)),
            dma((2, HEADS)),
            dma((2, HEADS)),
            dma((HEADS,)),
            dma((HEADS,)),
            dma((2,)),
        ],
        compiler_params=pltpu.CompilerParams(
            collective_id=0, has_side_effects=True, vmem_limit_bytes=40 * 1024 * 1024
        ),
    )(tokens[0], queries[0], master, grad, moment, second, cosine, sine)
    return (new_master, new_moment, new_second, codes, attended[None])


def solution(mesh):
    rows = P(("dp", "ctx"), None)
    return jax.shard_map(
        on_device,
        mesh=mesh,
        in_specs=(P("dp", "ctx", None), P("dp", "ctx", None), rows, rows, rows, rows),
        out_specs=(rows, rows, rows, rows, P("dp", "ctx", None)),
        check_vma=False,
    )
```

```python
import functools

import jax
import jax.numpy as jnp
from jax import lax
from jax.experimental import pallas as pl
from jax.experimental.pallas import tpu as pltpu
from jax.sharding import PartitionSpec as P

HD = 128
KVH = 8
WINDOW = 512
GROUP = 2
ROWS = 256
WIDTH = 3072
KVW = 2048

beta_one = 0.9
beta_two = 0.95
adam_eps = 1e-08
decay_rate = 0.1
learn_rate = 0.001
step_count = 1000
soft_cap = 50.0
rope_base = 10000.0

MESH = pl.DeviceIdType.MESH
HEADS = 4
LOG2E = 1.4426950408889634


PROJECT, LATE, ATTEND, START = 4, 5, 6, 7


def listed(text):
    kinds = {"0": 0, "1": 1, "2": 2, "3": 3, "P": PROJECT, "L": LATE, "A": ATTEND, "S": START}
    return [4 * kinds[item[0]] + int(item[1]) for item in text.split()]


ORDER = listed("S0 S1 00 S2") + listed("01 S3 10 11") + listed("20 02 21 30")
ORDER += listed("12 31 P0 03") + listed("22 13 P1 L0") + listed("32 23 P2 L1")
ORDER += listed("33 A0 P3 L2") + listed("A1 L3 A2 A3")


def rem(a, b):
    return lax.rem(a, jnp.int32(b))


def div(a, b):
    return lax.div(a, jnp.int32(b))


def kernel(
    tok_hbm, q_hbm, master_hbm, grad_hbm, moment_hbm, second_hbm, cosine, sine,
    attended, new_master, new_moment, new_second, codes,
    weights, tok, qs, keyval, relay, detour, sent_out, state, staged, pieces, block, peaks,
    tok_sem, q_sem, state_sem, piece_sem, x_send, x_recv, first_send, first_recv,
    ring_send, ring_recv, early_send, late_send, near_recv, far_recv, relay_recv, detour_recv,
    out_send, out_recv, peak_sem,
):
    dp, ctx = lax.axis_index("dp"), lax.axis_index("ctx")
    core, y, z_lo = rem(dp, 2), rem(div(dp, 2), 8), div(dp, 16)
    x, z_hi = rem(ctx, 4), div(ctx, 4)
    z = 2 * z_hi + z_lo
    kind, half = div(z_hi, 2), rem(z_hi, 2)
    row_group = (z_lo * 8 + y) * 2

    def device(xx, yy, zz):
        return ((rem(zz, 2) * 8 + yy) * 2 + core, div(zz, 2) * 4 + xx)

    sibling = (row_group + 1 - core, ctx)
    loads = [
        pltpu.make_async_copy(ref, state.at[i], state_sem.at[i])
        for i, ref in enumerate((master_hbm, grad_hbm, moment_hbm, second_hbm))
    ]
    for load in loads:
        load.start()
    barrier = pltpu.get_barrier_semaphore()

    def greet(i, _):
        to_core, to_ctx = rem(i, 2), div(i, 2)

        @pl.when((to_core != core) | (to_ctx != ctx))
        def _():
            pl.semaphore_signal(
                barrier, inc=1, device_id=(row_group + to_core, to_ctx), device_id_type=MESH
            )

        return 0

    lax.fori_loop(0, 32, greet, 0)

    def greet_y(k, _):
        pl.semaphore_signal(
            barrier, inc=1, device_id=device(x, rem(y + k, 8), z), device_id_type=MESH
        )
        return 0

    lax.fori_loop(1, 8, greet_y, 0)

    def greet_z(k, _):
        pl.semaphore_signal(
            barrier, inc=1, device_id=device(x, y, rem(z + 2 * k + 1, 8)), device_id_type=MESH
        )
        return 0

    lax.fori_loop(0, 4, greet_z, 0)

    own_cols = pl.ds(pl.multiple_of(core * 1024, 1024), 1024)
    their_cols = pl.ds(pl.multiple_of((1 - core) * 1024, 1024), 1024)
    own_tok = pltpu.make_async_copy(tok_hbm, tok.at[0], tok_sem.at[0])
    own_q = pltpu.make_async_copy(q_hbm.at[:, own_cols], qs.at[0], q_sem.at[0])
    own_tok.start()
    own_q.start()

    for load in loads:
        load.wait()
    old, g = state[0], state[1]
    mom = beta_one * state[2] + (1.0 - beta_one) * g
    sec = beta_two * state[3] + (1.0 - beta_two) * g * g
    mom_hat = mom / (1.0 - beta_one**step_count)
    sec_hat = sec / (1.0 - beta_two**step_count)
    update = mom_hat / (jnp.sqrt(sec_hat) + adam_eps) + decay_rate * old
    fresh = old - learn_rate * update
    new_master[...] = fresh
    new_moment[...] = mom
    new_second[...] = sec
    staged[...] = jnp.zeros_like(staged)
    for b in range(16):
        staged[b, 0:6, :] = fresh[:, 128 * b : 128 * b + 128]

    pl.semaphore_wait(barrier, 42)

    def owner(b):
        head = rem(b, 8)
        return div(head, 4), (div(b, 8) * 2 + core) * 4 + rem(head, 4)

    def send_piece(b, _):
        to_core, to_ctx = owner(b)
        mine = (to_core == core) & (to_ctx == ctx)

        @pl.when(mine)
        def _():
            pltpu.make_async_copy(staged.at[b], pieces.at[ctx], piece_sem.at[1]).start()

        @pl.when(jnp.logical_not(mine))
        def _():
            pltpu.make_async_remote_copy(
                src_ref=staged.at[b],
                dst_ref=pieces.at[ctx],
                send_sem=piece_sem.at[0],
                recv_sem=piece_sem.at[1],
                device_id=(row_group + to_core, to_ctx),
                device_id_type=MESH,
            ).start()

        return 0

    lax.fori_loop(0, 16, send_piece, 0)
    pltpu.make_async_copy(pieces, pieces, piece_sem.at[1]).wait()

    for j in range(16):
        block[6 * j : 6 * j + 6, :] = pieces[j, 0:6, :]
    weights[x, kind, z_lo, y, half] = block[...].astype(jnp.bfloat16)

    def x_copy(k):
        ref = weights.at[x, kind, z_lo, y, half]
        return pltpu.make_async_remote_copy(
            src_ref=ref, dst_ref=ref, send_sem=x_send.at[k], recv_sem=x_recv.at[k],
            device_id=device(rem(x + k + 1, 4), y, z), device_id_type=MESH,
        )

    for k in range(3):
        x_copy(k).start()

    their_tok = pltpu.make_async_remote_copy(
        src_ref=tok_hbm, dst_ref=tok.at[1], send_sem=tok_sem.at[1], recv_sem=tok_sem.at[2],
        device_id=sibling, device_id_type=MESH,
    )
    their_q = pltpu.make_async_remote_copy(
        src_ref=q_hbm.at[:, their_cols], dst_ref=qs.at[1], send_sem=q_sem.at[1],
        recv_sem=q_sem.at[2], device_id=sibling, device_id_type=MESH,
    )
    their_tok.start()
    their_q.start()

    for k in range(3):
        ref = weights.at[rem(x + 3 - k, 4), kind, z_lo, y, half]
        pltpu.make_async_copy(ref, ref, x_recv.at[k]).wait()

    def first(h):
        upper = weights.at[h, kind, z_lo, y, half, pl.ds(0, 48), :]
        lower = weights.at[h, kind, z_lo, y, half, pl.ds(48, 48), :]

        def to_peer(k, _):
            pltpu.make_async_remote_copy(
                src_ref=upper, dst_ref=upper, send_sem=first_send.at[0, h],
                recv_sem=first_recv.at[0, h],
                device_id=device(x, rem(y + k, 8), z), device_id_type=MESH,
            ).start()
            pltpu.make_async_remote_copy(
                src_ref=lower, dst_ref=lower, send_sem=first_send.at[1, h],
                recv_sem=first_recv.at[1, h],
                device_id=device(x, y, rem(z + k, 8)), device_id_type=MESH,
            ).start()
            return 0

        lax.fori_loop(1, 8, to_peer, 0)

    def wait_first(sems, h):
        for axis in range(2):
            ref = weights.at[h, 0, 0, pl.ds(0, 7), 0, pl.ds(0, 48), :]
            pltpu.make_async_copy(ref, ref, sems.at[axis, h]).wait()

    def part(axis, h, at, which):
        if axis == 0:
            rows = (pl.ds(0, 8), pl.ds(0, 4), pl.ds(4, 4))[which]
            return weights.at[
                h, div(at, 4), rem(at, 2), rows, rem(div(at, 2), 2), pl.ds(0, 48), :
            ]
        kinds = (pl.ds(0, 2), pl.ds(0, 1), pl.ds(1, 1))[which]
        return weights.at[h, kinds, :, at, :, pl.ds(48, 48), :]

    def ring_copy(axis, way, h, step, received, last):
        here = (z, y)[axis]
        sign = 1 - 2 * way
        origin = rem(here - sign * (step + (1 if received else 0)) + 16, 8)
        which = 1 + way if last else 0
        target = rem(here + sign + 8, 8)
        ref = part(axis, h, origin, which)
        return pltpu.make_async_remote_copy(
            src_ref=ref, dst_ref=ref, send_sem=ring_send.at[axis, way, h, step],
            recv_sem=ring_recv.at[axis, way, h, step],
            device_id=device(x, y, target) if axis == 0 else device(x, target, z),
            device_id_type=MESH,
        )

    def ring_start(h, step, last):
        for axis in range(2):
            for way in range(2):
                ring_copy(axis, way, h, step, False, last).start()

    def ring_wait(h, step, last):
        for axis in range(2):
            for way in range(2):
                ring_copy(axis, way, h, step, True, last).wait_recv()

    def project(h):
        total = jnp.zeros((2 * ROWS, 2 * HD), jnp.float32)
        top = jnp.zeros((8, 2 * HD), jnp.float32)
        for c in range(4):
            low = weights[h, 0, c // 2, 4 * (c % 2) : 4 * (c % 2) + 4].reshape(768, HD)
            high = weights[h, 1, c // 2, 4 * (c % 2) : 4 * (c % 2) + 4].reshape(768, HD)
            both = jnp.concatenate([low, high], axis=1)
            rows = tok[:, :, 768 * c : 768 * c + 768].reshape(2 * ROWS, 768)
            total = total + jnp.dot(rows, both, preferred_element_type=jnp.float32)
            size = jnp.abs(both.astype(jnp.float32)).reshape(96, 8, 2 * HD)
            top = jnp.maximum(top, jnp.max(size, axis=0))
        top = jnp.broadcast_to(jnp.max(top, axis=0, keepdims=True), (8, 2 * HD))
        peaks[core, h, 0] = top[:, :HD]
        peaks[core, h, 1] = top[:, HD:]
        keys = total[:, :HD]
        turned = pltpu.roll(keys, 64, 1)
        for s in range(2):
            span = slice(ROWS * s, ROWS * s + ROWS)
            rotated = keys[span] * cosine[...] + turned[span] * sine[...]
            keyval[h, s, 0, 512:768, :] = rotated.astype(jnp.bfloat16)
            keyval[h, s, 1, 512:768, :] = total[span, HD:].astype(jnp.bfloat16)

    def slot(h, s, n):
        return keyval.at[h, s, :, pl.ds(256 * n, 256), :]

    def place(xx, up):
        return (dp, rem(z_hi + up, 4) * 4 + xx)

    def send(src, dst, send_sem, recv_sem, to):
        pltpu.make_async_remote_copy(
            src_ref=src, dst_ref=dst, send_sem=send_sem, recv_sem=recv_sem,
            device_id=to, device_id_type=MESH,
        ).start()

    def near(src, h, s, sem, to):
        send(src, slot(h, s, 1), sem, near_recv.at[h, s], to)

    def far(src, h, s, sem, to):
        send(src, slot(h, s, 0), sem, far_recv.at[h, s], to)

    def early(h):
        sem = early_send.at[h]

        @pl.when(x == 3)
        def _():
            send(slot(h, 0, 2), relay.at[h], sem, relay_recv.at[h], place(3, 1))
            send(slot(h, 1, 2), relay.at[h], sem, relay_recv.at[h], place(0, 0))

        @pl.when(x == 2)
        def _():
            far(slot(h, 0, 2), h, 0, sem, place(0, 1))
            send(slot(h, 1, 2), relay.at[h], sem, relay_recv.at[h], place(1, 0))

        @pl.when(x < 3)
        def _():
            for s in range(2):
                near(slot(h, s, 2), h, s, sem, place(x + 1, 0))

        @pl.when(x == 1)
        def _():
            for s in range(2):
                far(slot(h, s, 2), h, s, sem, place(3, 0))

        @pl.when(x == 0)
        def _():
            send(slot(h, 1, 2), detour.at[h], sem, detour_recv.at[h], place(3, 0))

    def wait_slot(sems, h, s, n):
        pltpu.make_async_copy(slot(h, s, n), slot(h, s, n), sems.at[h, s]).wait()

    def late(h):
        sem = late_send.at[h]

        @pl.when(x != 2)
        def _():
            pltpu.make_async_copy(relay.at[h], relay.at[h], relay_recv.at[h]).wait()

        @pl.when(x == 0)
        def _():
            near(relay.at[h], h, 1, sem, place(0, 1))

        @pl.when(x == 1)
        def _():
            far(relay.at[h], h, 1, sem, place(0, 1))
            wait_slot(near_recv, h, 0, 1)
            far(slot(h, 0, 1), h, 0, sem, place(2, 0))

        @pl.when(x == 3)
        def _():
            near(relay.at[h], h, 0, sem, place(0, 0))
            far(relay.at[h], h, 0, sem, place(1, 0))
            pltpu.make_async_copy(detour.at[h], detour.at[h], detour_recv.at[h]).wait()
            far(detour.at[h], h, 1, sem, place(2, 0))

    def wait_halo(h):
        wait_slot(near_recv, h, 1, 1)

        @pl.when(x == 0)
        def _():
            far(slot(h, 1, 1), h, 1, late_send.at[h], place(1, 0))

        @pl.when(x != 1)
        def _():
            wait_slot(near_recv, h, 0, 1)

        for s in range(2):
            wait_slot(far_recv, h, s, 0)

    def wait_sent(sem, n):
        ref = keyval.at[0, :, :, pl.ds(0, 128 * n), :]
        pltpu.make_async_copy(ref, ref, sem).wait()

    def halo_sent(h):
        @pl.when(x == 0)
        def _():
            wait_sent(early_send.at[h], 3)
            wait_sent(late_send.at[h], 2)

        @pl.when(x == 1)
        def _():
            wait_sent(early_send.at[h], 4)
            wait_sent(late_send.at[h], 2)

        @pl.when(x == 2)
        def _():
            wait_sent(early_send.at[h], 4)

        @pl.when(x == 3)
        def _():
            wait_sent(early_send.at[h], 2)
            wait_sent(late_send.at[h], 3)

    row_id = lax.broadcasted_iota(jnp.int32, (2 * 128, 128), 0)
    row_id = jnp.where(row_id >= 128, row_id - 128, row_id)
    col_id = lax.broadcasted_iota(jnp.int32, (2 * 128, 128), 1)
    past = col_id > row_id

    def attend(h):
        def one(i, _):
            s, a = div(i, 2), rem(i, 2)
            start = pl.multiple_of(a * 128, 128)
            cols = pl.ds(pl.multiple_of(h * 256, 256), 256)
            q = qs[s, pl.ds(start, 128), cols]
            q = jnp.concatenate([q[:, :HD], q[:, HD:]], axis=0)
            keys = keyval[h, s, 0, pl.ds(start, 640), :]
            values = keyval[h, s, 1, pl.ds(start, 640), :]
            scores = lax.dot_general(
                q, keys, (((1,), (1,)), ((), ())), preferred_element_type=jnp.float32
            )
            weight = jnp.exp2(jnp.tanh(scores * (1.0 / 600.0)) * (soft_cap * LOG2E))
            tiles = []
            for t in range(5):
                tile = weight[:, 128 * t : 128 * t + 128]
                inside = (128 * t - 512 + ctx * 256 + start) >= 0
                if t == 0:
                    tile = jnp.where(past & inside, tile, 0.0)
                elif t == 4:
                    tile = jnp.where(past, 0.0, tile)
                else:
                    tile = jnp.where(inside, tile, 0.0)
                tiles.append(tile)
            norm = jnp.sum(tiles[0] + tiles[1] + tiles[2] + tiles[3] + tiles[4], axis=1, keepdims=True)
            weight = jnp.concatenate([t.astype(jnp.bfloat16) for t in tiles], axis=1)
            mixed = jnp.dot(weight, values, preferred_element_type=jnp.float32)
            mixed = (mixed / norm).astype(jnp.bfloat16)
            mixed = jnp.concatenate([mixed[:128], mixed[128:]], axis=1)

            @pl.when(s == 0)
            def _():
                out_cols = pl.ds(pl.multiple_of(core * 1024 + h * 256, 256), 256)
                attended[pl.ds(start, 128), out_cols] = mixed

            @pl.when(s == 1)
            def _():
                sent_out[h, pl.ds(start, 128), :] = mixed

            return 0

        lax.fori_loop(0, 4, one, 0)

    def out_copy(h):
        out_cols = pl.ds(pl.multiple_of(core * 1024 + h * 256, 256), 256)
        return pltpu.make_async_remote_copy(
            src_ref=sent_out.at[h], dst_ref=attended.at[:, out_cols],
            send_sem=out_send.at[h], recv_sem=out_recv.at[h],
            device_id=sibling, device_id_type=MESH,
        )


    def event(e):
        h, kind_of = rem(e, 4), div(e, 4)

        @pl.when(kind_of == START)
        def _():
            first(h)

        @pl.when(kind_of == 0)
        def _():
            wait_first(first_recv, h)

        @pl.when((kind_of >= 1) & (kind_of < 4))
        def _():
            ring_wait(h, kind_of - 1, False)

        @pl.when(kind_of < 3)
        def _():
            ring_start(h, kind_of, False)

        @pl.when(kind_of == 3)
        def _():
            ring_start(h, 3, True)

        @pl.when(kind_of == PROJECT)
        def _():
            ring_wait(h, 3, True)

            @pl.when(h == 0)
            def _():
                own_tok.wait()
                their_tok.wait()

            project(h)
            early(h)

        @pl.when(kind_of == LATE)
        def _():
            late(h)

        @pl.when(kind_of == ATTEND)
        def _():
            wait_halo(h)

            @pl.when(h == 0)
            def _():
                own_q.wait()
                their_q.wait()

            attend(h)
            out_copy(h).start()

    def group(i, _):
        word = jnp.int32(0)
        for k in range(8):
            coded = 0
            for e in reversed(ORDER[4 * k : 4 * k + 4]):
                coded = coded * 32 + e
            word = jnp.where(i == k, jnp.int32(coded), word)

        def one(_, word):
            event(rem(word, 32))
            return div(word, 32)

        lax.fori_loop(0, 4, one, word)
        return 0

    lax.fori_loop(0, 8, group, 0)

    peak_copy = pltpu.make_async_remote_copy(
        src_ref=peaks.at[core], dst_ref=peaks.at[core], send_sem=peak_sem.at[0],
        recv_sem=peak_sem.at[1], device_id=sibling, device_id_type=MESH,
    )
    peak_copy.start()

    @pl.when(half == core)
    def _():
        ref = staged.at[pl.ds(0, 15)]
        pltpu.make_async_copy(ref, ref, piece_sem.at[0]).wait()

    @pl.when(half != core)
    def _():
        pltpu.make_async_copy(staged, staged, piece_sem.at[0]).wait()

    for k in range(3):
        x_copy(k).wait_send()

    def drain(h, _):
        wait_first(first_send, h)
        for step in range(4):
            for axis in range(2):
                for way in range(2):
                    ring_copy(axis, way, h, step, False, step == 3).wait_send()
        halo_sent(h)
        out_copy(h).wait_send()
        theirs = pl.ds(pl.multiple_of((1 - core) * 1024 + h * 256, 256), 256)
        ref = attended.at[:, theirs]
        pltpu.make_async_copy(ref, ref, out_recv.at[h]).wait()
        return 0

    lax.fori_loop(0, HEADS, drain, 0)

    peak_copy.wait_send()
    ref = peaks.at[1 - core]
    pltpu.make_async_copy(ref, ref, peak_sem.at[1]).wait()
    for b in range(16):
        head = b % 8
        peak = peaks[head // 4, head % 4, b // 8, 0:1, :] + 1e-06
        codes[:, 128 * b : 128 * b + 128] = (staged[b, 0:6, :] / peak).astype(jnp.bfloat16)


def on_device(tokens, queries, master, grad, moment, second):
    query_start = lax.axis_index("ctx") * ROWS
    positions = query_start + jnp.arange(ROWS, dtype=jnp.int32)
    freqs = rope_base ** (-jnp.arange(HD // 2, dtype=jnp.float32) * 2.0 / HD)
    angles = positions.astype(jnp.float32)[:, None] * freqs[None, :]
    cosine, sine = jnp.cos(angles), jnp.sin(angles)
    cosine = jnp.concatenate([cosine, cosine], axis=1)
    sine = jnp.concatenate([-sine, sine], axis=1)
    vmem = pl.BlockSpec(memory_space=pltpu.VMEM)
    hbm = pl.BlockSpec(memory_space=pl.ANY)
    dma = pltpu.SemaphoreType.DMA
    f32, bf16 = jnp.float32, jnp.bfloat16
    attended, new_master, new_moment, new_second, codes = pl.pallas_call(
        kernel,
        out_shape=(
            jax.ShapeDtypeStruct((ROWS, KVW), bf16),
            jax.ShapeDtypeStruct((6, KVW), f32),
            jax.ShapeDtypeStruct((6, KVW), f32),
            jax.ShapeDtypeStruct((6, KVW), f32),
            jax.ShapeDtypeStruct((6, KVW), bf16),
        ),
        in_specs=[hbm] * 6 + [vmem] * 2,
        out_specs=(vmem,) * 5,
        scratch_shapes=[
            pltpu.VMEM((HEADS, 2, 2, 8, 2, 96, HD), bf16),
            pltpu.VMEM((2, ROWS, WIDTH), bf16),
            pltpu.VMEM((2, ROWS, 1024), bf16),
            pltpu.VMEM((HEADS, 2, 2, 768, HD), bf16),
            pltpu.VMEM((HEADS, 2, ROWS, HD), bf16),
            pltpu.VMEM((HEADS, 2, ROWS, HD), bf16),
            pltpu.VMEM((HEADS, ROWS, 256), bf16),
            pltpu.VMEM((4, 6, KVW), f32),
            pltpu.VMEM((16, 8, 128), f32),
            pltpu.VMEM((16, 8, 128), f32),
            pltpu.VMEM((96, 128), f32),
            pltpu.VMEM((2, HEADS, 2, 8, 128), f32),
            dma((3,)),
            dma((3,)),
            dma((4,)),
            dma((2,)),
            dma((3,)),
            dma((3,)),
            dma((2, HEADS)),
            dma((2, HEADS)),
            dma((2, 2, HEADS, 4)),
            dma((2, 2, HEADS, 4)),
            dma((HEADS,)),
            dma((HEADS,)),
            dma((HEADS, 2)),
            dma((HEADS, 2)),
            dma((HEADS,)),
            dma((HEADS,)),
            dma((HEADS,)),
            dma((HEADS,)),
            dma((2,)),
        ],
        compiler_params=pltpu.CompilerParams(
            collective_id=0, has_side_effects=True, vmem_limit_bytes=56 * 1024 * 1024
        ),
    )(tokens[0], queries[0], master, grad, moment, second, cosine, sine)
    return (new_master, new_moment, new_second, codes, attended[None])


def solution(mesh):
    rows = P(("dp", "ctx"), None)
    return jax.shard_map(
        on_device,
        mesh=mesh,
        in_specs=(P("dp", "ctx", None), P("dp", "ctx", None), rows, rows, rows, rows),
        out_specs=(rows, rows, rows, rows, P("dp", "ctx", None)),
        check_vma=False,
    )
```

```python
import jax
import jax.numpy as jnp
from jax import lax
from jax.experimental import pallas as pl
from jax.experimental.pallas import tpu as pltpu
from jax.sharding import PartitionSpec as P

HD = 128
KVH = 8
WINDOW = 512
GROUP = 2
ROWS = 256
WIDTH = 3072
KVW = 2048

beta_one = 0.9
beta_two = 0.95
adam_eps = 1e-08
decay_rate = 0.1
learn_rate = 0.001
step_count = 1000
soft_cap = 50.0
rope_base = 10000.0

MESH = pl.DeviceIdType.MESH
LIMIT = 52
HEADS = 4
LOG2E = 1.4426950408889634


PROJECT, LATE, ATTEND, START = 4, 5, 6, 7


def listed(text):
    kinds = {"0": 0, "1": 1, "2": 2, "3": 3, "P": PROJECT, "L": LATE, "A": ATTEND, "S": START}
    return [4 * kinds[item[0]] + int(item[1]) for item in text.split()]


ORDER = listed('S0 S1 00 S2')
ORDER += listed('01 S3 10 11')
ORDER += listed('20 02 21 30')
ORDER += listed('12 31 P0 03')
ORDER += listed('22 13 P1 L0')
ORDER += listed('32 23 P2 L1')
ORDER += listed('33 A0 P3 L2')
ORDER += listed('A1 L3 A2 A3')


def rem(a, b):
    return lax.rem(a, jnp.int32(b))


def div(a, b):
    return lax.div(a, jnp.int32(b))


def kernel(
    tok_hbm, q_hbm, fresh, cosine, sine,
    attended, peak_out,
    along_z, along_y, tok, qs, keyval, relay, detour, sent_out, staged, pieces, block, peaks,
    tok_sem, q_sem, piece_sem, x_send, x_recv, first_send, first_recv,
    ring_send, ring_recv, early_send, late_send, near_recv, far_recv, relay_recv, detour_recv,
    out_send, out_recv, peak_sem,
):
    dp, ctx = lax.axis_index("dp"), lax.axis_index("ctx")
    core, y, z_lo = rem(dp, 2), rem(div(dp, 2), 8), div(dp, 16)
    x, z_hi = rem(ctx, 4), div(ctx, 4)
    z = 2 * z_hi + z_lo
    kind, half = div(z_hi, 2), rem(z_hi, 2)
    row_group = (z_lo * 8 + y) * 2

    def device(xx, yy, zz):
        return ((rem(zz, 2) * 8 + yy) * 2 + core, div(zz, 2) * 4 + xx)

    sibling = (row_group + 1 - core, ctx)
    barrier = pltpu.get_barrier_semaphore()

    def greet(i, _):
        to_core, to_ctx = rem(i, 2), div(i, 2)

        @pl.when((to_core != core) | (to_ctx != ctx))
        def _():
            pl.semaphore_signal(
                barrier, inc=1, device_id=(row_group + to_core, to_ctx), device_id_type=MESH
            )

        return 0

    lax.fori_loop(0, 32, greet, 0)

    def greet_y(k, _):
        pl.semaphore_signal(
            barrier, inc=1, device_id=device(x, rem(y + k, 8), z), device_id_type=MESH
        )
        return 0

    lax.fori_loop(1, 8, greet_y, 0)

    def greet_z(k, _):
        pl.semaphore_signal(
            barrier, inc=1, device_id=device(x, y, rem(z + 2 * k + 1, 8)), device_id_type=MESH
        )
        return 0

    lax.fori_loop(0, 4, greet_z, 0)

    own_cols = pl.ds(pl.multiple_of(core * 1024, 1024), 1024)
    their_cols = pl.ds(pl.multiple_of((1 - core) * 1024, 1024), 1024)
    own_tok = pltpu.make_async_copy(tok_hbm, tok.at[0], tok_sem.at[0])
    own_q = pltpu.make_async_copy(q_hbm.at[:, own_cols], qs.at[0], q_sem.at[0])
    own_tok.start()
    own_q.start()

    staged[...] = jnp.zeros_like(staged)
    for b in range(16):
        staged[b, 0:6, :] = fresh[:, 128 * b : 128 * b + 128]

    pl.semaphore_wait(barrier, 42)

    def owner(b):
        head = rem(b, 8)
        return div(head, 4), (div(b, 8) * 2 + core) * 4 + rem(head, 4)

    def send_piece(b, _):
        to_core, to_ctx = owner(b)
        mine = (to_core == core) & (to_ctx == ctx)

        @pl.when(mine)
        def _():
            pltpu.make_async_copy(staged.at[b], pieces.at[ctx], piece_sem.at[1]).start()

        @pl.when(jnp.logical_not(mine))
        def _():
            pltpu.make_async_remote_copy(
                src_ref=staged.at[b],
                dst_ref=pieces.at[ctx],
                send_sem=piece_sem.at[0],
                recv_sem=piece_sem.at[1],
                device_id=(row_group + to_core, to_ctx),
                device_id_type=MESH,
            ).start()

        return 0

    lax.fori_loop(0, 16, send_piece, 0)
    pltpu.make_async_copy(pieces, pieces, piece_sem.at[1]).wait()

    for j in range(16):
        block[6 * j : 6 * j + 6, :] = pieces[j, 0:6, :]
    along_z[x, z, y] = block[0:48, :].astype(jnp.bfloat16)
    along_y[x, y, z] = block[48:96, :].astype(jnp.bfloat16)

    def x_copy(k, which):
        ref = (along_z.at[x, z, y], along_y.at[x, y, z])[which]
        return pltpu.make_async_remote_copy(
            src_ref=ref, dst_ref=ref, send_sem=x_send.at[which, k], recv_sem=x_recv.at[which, k],
            device_id=device(rem(x + k + 1, 4), y, z), device_id_type=MESH,
        )

    for k in range(3):
        x_copy(k, 0).start()
        x_copy(k, 1).start()

    their_tok = pltpu.make_async_remote_copy(
        src_ref=tok_hbm, dst_ref=tok.at[1], send_sem=tok_sem.at[1], recv_sem=tok_sem.at[2],
        device_id=sibling, device_id_type=MESH,
    )
    their_q = pltpu.make_async_remote_copy(
        src_ref=q_hbm.at[:, their_cols], dst_ref=qs.at[1], send_sem=q_sem.at[1],
        recv_sem=q_sem.at[2], device_id=sibling, device_id_type=MESH,
    )
    their_tok.start()
    their_q.start()

    for k in range(3):
        origin = rem(x + 3 - k, 4)
        for which, ref in enumerate((along_z.at[origin, z, y], along_y.at[origin, y, z])):
            pltpu.make_async_copy(ref, ref, x_recv.at[which, k]).wait()

    def first(h):
        upper = along_z.at[h, z, y]
        lower = along_y.at[h, y, z]

        def to_peer(k, _):
            pltpu.make_async_remote_copy(
                src_ref=upper, dst_ref=upper, send_sem=first_send.at[0, h],
                recv_sem=first_recv.at[0, h],
                device_id=device(x, rem(y + k, 8), z), device_id_type=MESH,
            ).start()
            pltpu.make_async_remote_copy(
                src_ref=lower, dst_ref=lower, send_sem=first_send.at[1, h],
                recv_sem=first_recv.at[1, h],
                device_id=device(x, y, rem(z + k, 8)), device_id_type=MESH,
            ).start()
            return 0

        lax.fori_loop(1, 8, to_peer, 0)

    def wait_first(sems, h):
        for axis in range(2):
            ref = along_z.at[h, 0, pl.ds(0, 7)]
            pltpu.make_async_copy(ref, ref, sems.at[axis, h]).wait()

    def part(axis, h, at, which):
        return (along_z, along_y)[axis].at[h, at, (pl.ds(0, 8), pl.ds(0, 4), pl.ds(4, 4))[which]]

    def ring_copy(axis, way, h, step, received, last):
        here = (z, y)[axis]
        sign = 1 - 2 * way
        origin = rem(here - sign * (step + (1 if received else 0)) + 16, 8)
        which = 1 + way if last else 0
        target = rem(here + sign + 8, 8)
        ref = part(axis, h, origin, which)
        return pltpu.make_async_remote_copy(
            src_ref=ref, dst_ref=ref, send_sem=ring_send.at[axis, way, h, step],
            recv_sem=ring_recv.at[axis, way, h, step],
            device_id=device(x, y, target) if axis == 0 else device(x, target, z),
            device_id_type=MESH,
        )

    def ring_start(h, step, last):
        for axis in range(2):
            for way in range(2):
                ring_copy(axis, way, h, step, False, last).start()

    def ring_wait(h, step, last):
        for axis in range(2):
            for way in range(2):
                ring_copy(axis, way, h, step, True, last).wait_recv()

    def project(h):
        total = jnp.zeros((2 * ROWS, 2 * HD), jnp.float32)
        top = jnp.zeros((8, 2 * HD), jnp.float32)
        for c in range(4):
            sides = []
            for kv in range(2):
                strips = []
                for yy in range(4 * (c % 2), 4 * (c % 2) + 4):
                    for zz in (4 * kv + c // 2, 4 * kv + 2 + c // 2):
                        strips += [along_z[h, zz, yy], along_y[h, yy, zz]]
                sides.append(jnp.concatenate(strips, axis=0))
            both = jnp.concatenate(sides, axis=1)
            rows = tok[:, :, 768 * c : 768 * c + 768].reshape(2 * ROWS, 768)
            total = total + jnp.dot(rows, both, preferred_element_type=jnp.float32)
            size = jnp.abs(both.astype(jnp.float32)).reshape(96, 8, 2 * HD)
            top = jnp.maximum(top, jnp.max(size, axis=0))
        top = jnp.broadcast_to(jnp.max(top, axis=0, keepdims=True), (8, 2 * HD))
        peaks[core, h, 0] = top[:, :HD]
        peaks[core, h, 1] = top[:, HD:]
        keys = total[:, :HD]
        turned = pltpu.roll(keys, 64, 1)
        for s in range(2):
            span = slice(ROWS * s, ROWS * s + ROWS)
            rotated = keys[span] * cosine[...] + turned[span] * sine[...]
            keyval[h, s, 0, 512:768, :] = rotated.astype(jnp.bfloat16)
            keyval[h, s, 1, 512:768, :] = total[span, HD:].astype(jnp.bfloat16)

    def slot(h, s, n):
        return keyval.at[h, s, :, pl.ds(256 * n, 256), :]

    def place(xx, up):
        return (dp, rem(z_hi + up, 4) * 4 + xx)

    def send(src, dst, send_sem, recv_sem, to):
        pltpu.make_async_remote_copy(
            src_ref=src, dst_ref=dst, send_sem=send_sem, recv_sem=recv_sem,
            device_id=to, device_id_type=MESH,
        ).start()

    def near(src, h, s, sem, to):
        send(src, slot(h, s, 1), sem, near_recv.at[h, s], to)

    def far(src, h, s, sem, to):
        send(src, slot(h, s, 0), sem, far_recv.at[h, s], to)

    def early(h):
        sem = early_send.at[h]

        @pl.when(x == 3)
        def _():
            send(slot(h, 0, 2), relay.at[h], sem, relay_recv.at[h], place(3, 1))
            send(slot(h, 1, 2), relay.at[h], sem, relay_recv.at[h], place(0, 0))

        @pl.when(x == 2)
        def _():
            far(slot(h, 0, 2), h, 0, sem, place(0, 1))
            send(slot(h, 1, 2), relay.at[h], sem, relay_recv.at[h], place(1, 0))

        @pl.when(x < 3)
        def _():
            for s in range(2):
                near(slot(h, s, 2), h, s, sem, place(x + 1, 0))

        @pl.when(x == 1)
        def _():
            for s in range(2):
                far(slot(h, s, 2), h, s, sem, place(3, 0))

        @pl.when(x == 0)
        def _():
            send(slot(h, 1, 2), detour.at[h], sem, detour_recv.at[h], place(3, 0))

    def wait_slot(sems, h, s, n):
        pltpu.make_async_copy(slot(h, s, n), slot(h, s, n), sems.at[h, s]).wait()

    def late(h):
        sem = late_send.at[h]

        @pl.when(x != 2)
        def _():
            pltpu.make_async_copy(relay.at[h], relay.at[h], relay_recv.at[h]).wait()

        @pl.when(x == 0)
        def _():
            near(relay.at[h], h, 1, sem, place(0, 1))

        @pl.when(x == 1)
        def _():
            far(relay.at[h], h, 1, sem, place(0, 1))
            wait_slot(near_recv, h, 0, 1)
            far(slot(h, 0, 1), h, 0, sem, place(2, 0))

        @pl.when(x == 3)
        def _():
            near(relay.at[h], h, 0, sem, place(0, 0))
            far(relay.at[h], h, 0, sem, place(1, 0))
            pltpu.make_async_copy(detour.at[h], detour.at[h], detour_recv.at[h]).wait()
            far(detour.at[h], h, 1, sem, place(2, 0))

    def wait_halo(h):
        wait_slot(near_recv, h, 1, 1)

        @pl.when(x == 0)
        def _():
            far(slot(h, 1, 1), h, 1, late_send.at[h], place(1, 0))

        @pl.when(x != 1)
        def _():
            wait_slot(near_recv, h, 0, 1)

        for s in range(2):
            wait_slot(far_recv, h, s, 0)

    def wait_sent(sem, n):
        ref = keyval.at[0, :, :, pl.ds(0, 128 * n), :]
        pltpu.make_async_copy(ref, ref, sem).wait()

    def halo_sent(h):
        @pl.when(x == 0)
        def _():
            wait_sent(early_send.at[h], 3)
            wait_sent(late_send.at[h], 2)

        @pl.when(x == 1)
        def _():
            wait_sent(early_send.at[h], 4)
            wait_sent(late_send.at[h], 2)

        @pl.when(x == 2)
        def _():
            wait_sent(early_send.at[h], 4)

        @pl.when(x == 3)
        def _():
            wait_sent(early_send.at[h], 2)
            wait_sent(late_send.at[h], 3)

    row_id = lax.broadcasted_iota(jnp.int32, (2 * 128, 128), 0)
    row_id = jnp.where(row_id >= 128, row_id - 128, row_id)
    col_id = lax.broadcasted_iota(jnp.int32, (2 * 128, 128), 1)
    past = col_id > row_id

    def attend(h):
        def one(i, _):
            s, a = div(i, 2), rem(i, 2)
            start = pl.multiple_of(a * 128, 128)
            cols = pl.ds(pl.multiple_of(h * 256, 256), 256)
            q = qs[s, pl.ds(start, 128), cols]
            q = jnp.concatenate([q[:, :HD], q[:, HD:]], axis=0)
            keys = keyval[h, s, 0, pl.ds(start, 640), :]
            values = keyval[h, s, 1, pl.ds(start, 640), :]
            scores = lax.dot_general(
                q, keys, (((1,), (1,)), ((), ())), preferred_element_type=jnp.float32
            )
            weight = jnp.exp2(jnp.tanh(scores * (1.0 / 600.0)) * (soft_cap * LOG2E))
            tiles = []
            for t in range(5):
                tile = weight[:, 128 * t : 128 * t + 128]
                inside = (128 * t - 512 + ctx * 256 + start) >= 0
                if t == 0:
                    tile = jnp.where(past & inside, tile, 0.0)
                elif t == 4:
                    tile = jnp.where(past, 0.0, tile)
                else:
                    tile = jnp.where(inside, tile, 0.0)
                tiles.append(tile)
            norm = jnp.sum(tiles[0] + tiles[1] + tiles[2] + tiles[3] + tiles[4], axis=1, keepdims=True)
            weight = jnp.concatenate([t.astype(jnp.bfloat16) for t in tiles], axis=1)
            mixed = jnp.dot(weight, values, preferred_element_type=jnp.float32)
            mixed = (mixed / norm).astype(jnp.bfloat16)
            mixed = jnp.concatenate([mixed[:128], mixed[128:]], axis=1)

            @pl.when(s == 0)
            def _():
                out_cols = pl.ds(pl.multiple_of(core * 1024 + h * 256, 256), 256)
                attended[pl.ds(start, 128), out_cols] = mixed

            @pl.when(s == 1)
            def _():
                sent_out[h, pl.ds(start, 128), :] = mixed

            return 0

        lax.fori_loop(0, 4, one, 0)

    def out_copy(h):
        out_cols = pl.ds(pl.multiple_of(core * 1024 + h * 256, 256), 256)
        return pltpu.make_async_remote_copy(
            src_ref=sent_out.at[h], dst_ref=attended.at[:, out_cols],
            send_sem=out_send.at[h], recv_sem=out_recv.at[h],
            device_id=sibling, device_id_type=MESH,
        )


    def event(e):
        h, kind_of = rem(e, 4), div(e, 4)

        @pl.when(kind_of == START)
        def _():
            first(h)

        @pl.when(kind_of == 0)
        def _():
            wait_first(first_recv, h)

        @pl.when((kind_of >= 1) & (kind_of < 4))
        def _():
            ring_wait(h, kind_of - 1, False)

        @pl.when(kind_of < 3)
        def _():
            ring_start(h, kind_of, False)

        @pl.when(kind_of == 3)
        def _():
            ring_start(h, 3, True)

        @pl.when(kind_of == PROJECT)
        def _():
            ring_wait(h, 3, True)

            @pl.when(h == 0)
            def _():
                own_tok.wait()
                their_tok.wait()

            project(h)
            early(h)

        @pl.when(kind_of == LATE)
        def _():
            late(h)

        @pl.when(kind_of == ATTEND)
        def _():
            wait_halo(h)

            @pl.when(h == 0)
            def _():
                own_q.wait()
                their_q.wait()

            attend(h)
            out_copy(h).start()

    def group(i, _):
        word = jnp.int32(0)
        for k in range(8):
            coded = 0
            for e in reversed(ORDER[4 * k : 4 * k + 4]):
                coded = coded * 32 + e
            word = jnp.where(i == k, jnp.int32(coded), word)

        def one(_, word):
            event(rem(word, 32))
            return div(word, 32)

        lax.fori_loop(0, 4, one, word)
        return 0

    lax.fori_loop(0, 8, group, 0)

    peak_copy = pltpu.make_async_remote_copy(
        src_ref=peaks.at[core], dst_ref=peaks.at[core], send_sem=peak_sem.at[0],
        recv_sem=peak_sem.at[1], device_id=sibling, device_id_type=MESH,
    )
    peak_copy.start()

    @pl.when(half == core)
    def _():
        ref = staged.at[pl.ds(0, 15)]
        pltpu.make_async_copy(ref, ref, piece_sem.at[0]).wait()

    @pl.when(half != core)
    def _():
        pltpu.make_async_copy(staged, staged, piece_sem.at[0]).wait()

    for k in range(3):
        x_copy(k, 0).wait_send()
        x_copy(k, 1).wait_send()

    def drain(h, _):
        wait_first(first_send, h)
        for step in range(4):
            for axis in range(2):
                for way in range(2):
                    ring_copy(axis, way, h, step, False, step == 3).wait_send()
        halo_sent(h)
        out_copy(h).wait_send()
        theirs = pl.ds(pl.multiple_of((1 - core) * 1024 + h * 256, 256), 256)
        ref = attended.at[:, theirs]
        pltpu.make_async_copy(ref, ref, out_recv.at[h]).wait()
        return 0

    lax.fori_loop(0, HEADS, drain, 0)

    peak_copy.wait_send()
    ref = peaks.at[1 - core]
    pltpu.make_async_copy(ref, ref, peak_sem.at[1]).wait()
    for b in range(16):
        head = b % 8
        peak_out[:, 128 * b : 128 * b + 128] = peaks[head // 4, head % 4, b // 8, 0:1, :] + 1e-06


def adamw(master, grad, moment, second):
    new_moment = beta_one * moment + (1.0 - beta_one) * grad
    new_second = beta_two * second + (1.0 - beta_two) * grad * grad
    moment_hat = new_moment / (1.0 - beta_one**step_count)
    second_hat = new_second / (1.0 - beta_two**step_count)
    update = moment_hat / (jnp.sqrt(second_hat) + adam_eps) + decay_rate * master
    return (master - learn_rate * update, new_moment, new_second)


def on_device(tokens, queries, master, grad, moment, second):
    new_master, new_moment, new_second = adamw(master, grad, moment, second)
    query_start = lax.axis_index("ctx") * ROWS
    positions = query_start + jnp.arange(ROWS, dtype=jnp.int32)
    freqs = rope_base ** (-jnp.arange(HD // 2, dtype=jnp.float32) * 2.0 / HD)
    angles = positions.astype(jnp.float32)[:, None] * freqs[None, :]
    cosine, sine = jnp.cos(angles), jnp.sin(angles)
    cosine = jnp.concatenate([cosine, cosine], axis=1)
    sine = jnp.concatenate([-sine, sine], axis=1)
    vmem = pl.BlockSpec(memory_space=pltpu.VMEM)
    hbm = pl.BlockSpec(memory_space=pl.ANY)
    dma = pltpu.SemaphoreType.DMA
    f32, bf16 = jnp.float32, jnp.bfloat16
    attended, peak = pl.pallas_call(
        kernel,
        out_shape=(
            jax.ShapeDtypeStruct((ROWS, KVW), bf16),
            jax.ShapeDtypeStruct((1, KVW), f32),
        ),
        in_specs=[hbm] * 2 + [vmem] * 3,
        out_specs=(vmem,) * 2,
        scratch_shapes=[
            pltpu.VMEM((HEADS, 8, 8, 48, HD), bf16),
            pltpu.VMEM((HEADS, 8, 8, 48, HD), bf16),
            pltpu.VMEM((2, ROWS, WIDTH), bf16),
            pltpu.VMEM((2, ROWS, 1024), bf16),
            pltpu.VMEM((HEADS, 2, 2, 768, HD), bf16),
            pltpu.VMEM((HEADS, 2, ROWS, HD), bf16),
            pltpu.VMEM((HEADS, 2, ROWS, HD), bf16),
            pltpu.VMEM((HEADS, ROWS, 256), bf16),
            pltpu.VMEM((16, 8, 128), f32),
            pltpu.VMEM((16, 8, 128), f32),
            pltpu.VMEM((96, 128), f32),
            pltpu.VMEM((2, HEADS, 2, 8, 128), f32),
            dma((3,)),
            dma((3,)),
            dma((2,)),
            dma((2, 3)),
            dma((2, 3)),
            dma((2, HEADS)),
            dma((2, HEADS)),
            dma((2, 2, HEADS, 4)),
            dma((2, 2, HEADS, 4)),
            dma((HEADS,)),
            dma((HEADS,)),
            dma((HEADS, 2)),
            dma((HEADS, 2)),
            dma((HEADS,)),
            dma((HEADS,)),
            dma((HEADS,)),
            dma((HEADS,)),
            dma((2,)),
        ],
        compiler_params=pltpu.CompilerParams(
            collective_id=0, has_side_effects=True, vmem_limit_bytes=LIMIT * 1024 * 1024
        ),
    )(tokens[0], queries[0], new_master, cosine, sine)
    codes = (new_master / peak).astype(bf16)
    return (new_master, new_moment, new_second, codes, attended[None])


def solution(mesh):
    rows = P(("dp", "ctx"), None)
    return jax.shard_map(
        on_device,
        mesh=mesh,
        in_specs=(P("dp", "ctx", None), P("dp", "ctx", None), rows, rows, rows, rows),
        out_specs=(rows, rows, rows, rows, P("dp", "ctx", None)),
        check_vma=False,
    )
```

```python
import jax
import jax.numpy as jnp
from jax import lax
from jax.experimental import pallas as pl
from jax.experimental.pallas import tpu as pltpu
from jax.sharding import PartitionSpec as P

HD = 128
KVH = 8
WINDOW = 512
GROUP = 2
ROWS = 256
WIDTH = 3072
KVW = 2048

beta_one = 0.9
beta_two = 0.95
adam_eps = 1e-08
decay_rate = 0.1
learn_rate = 0.001
step_count = 1000
soft_cap = 50.0
rope_base = 10000.0

MESH = pl.DeviceIdType.MESH
LIMIT = 52
HEADS = 4
LOG2E = 1.4426950408889634


PROJECT, LATE, ATTEND, START = 4, 5, 6, 7


def listed(text):
    kinds = {"0": 0, "1": 1, "2": 2, "3": 3, "P": PROJECT, "L": LATE, "A": ATTEND, "S": START}
    return [4 * kinds[item[0]] + int(item[1]) for item in text.split()]


ORDER = listed('S0 S1 00 S2')
ORDER += listed('01 S3 10 11')
ORDER += listed('20 02 21 30')
ORDER += listed('12 31 P0 03')
ORDER += listed('22 13 P1 L0')
ORDER += listed('32 23 P2 L1')
ORDER += listed('33 A0 P3 L2')
ORDER += listed('A1 L3 A2 A3')


def rem(a, b):
    return lax.rem(a, jnp.int32(b))


def div(a, b):
    return lax.div(a, jnp.int32(b))


def kernel(
    tok_hbm, q_hbm, fresh, cosine, sine,
    attended, peak_out,
    along_z, along_y, tok, qs, keyval, relay, detour, sent_out, staged, pieces, block, peaks,
    tok_sem, q_sem, piece_sem, x_send, x_recv, first_send, first_recv,
    ring_send, ring_recv, early_send, late_send, near_recv, far_recv, relay_recv, detour_recv,
    out_send, out_recv, peak_sem,
):
    dp, ctx = lax.axis_index("dp"), lax.axis_index("ctx")
    core, y, z_lo = rem(dp, 2), rem(div(dp, 2), 8), div(dp, 16)
    x, z_hi = rem(ctx, 4), div(ctx, 4)
    z = 2 * z_hi + z_lo
    kind, half = div(z_hi, 2), rem(z_hi, 2)
    row_group = (z_lo * 8 + y) * 2

    def device(xx, yy, zz):
        return ((rem(zz, 2) * 8 + yy) * 2 + core, div(zz, 2) * 4 + xx)

    sibling = (row_group + 1 - core, ctx)
    barrier = pltpu.get_barrier_semaphore()

    def greet(i, _):
        to_core, to_ctx = rem(i, 2), div(i, 2)

        @pl.when((to_core != core) | (to_ctx != ctx))
        def _():
            pl.semaphore_signal(
                barrier, inc=1, device_id=(row_group + to_core, to_ctx), device_id_type=MESH
            )

        return 0

    lax.fori_loop(0, 32, greet, 0)

    def greet_y(k, _):
        pl.semaphore_signal(
            barrier, inc=1, device_id=device(x, rem(y + k, 8), z), device_id_type=MESH
        )
        return 0

    lax.fori_loop(1, 8, greet_y, 0)

    def greet_z(k, _):
        pl.semaphore_signal(
            barrier, inc=1, device_id=device(x, y, rem(z + 2 * k + 1, 8)), device_id_type=MESH
        )
        return 0

    lax.fori_loop(0, 4, greet_z, 0)

    own_cols = pl.ds(pl.multiple_of(core * 1024, 1024), 1024)
    their_cols = pl.ds(pl.multiple_of((1 - core) * 1024, 1024), 1024)
    own_tok = pltpu.make_async_copy(tok_hbm, tok.at[0], tok_sem.at[0])
    own_q = pltpu.make_async_copy(q_hbm.at[:, own_cols], qs.at[0], q_sem.at[0])
    own_tok.start()
    own_q.start()

    staged[...] = jnp.zeros_like(staged)
    for b in range(16):
        staged[b, 0:6, :] = fresh[:, 128 * b : 128 * b + 128]

    pl.semaphore_wait(barrier, 42)

    def owner(b):
        head = rem(b, 8)
        return div(head, 4), (div(b, 8) * 2 + core) * 4 + rem(head, 4)

    def send_piece(b, _):
        to_core, to_ctx = owner(b)
        mine = (to_core == core) & (to_ctx == ctx)

        @pl.when(mine)
        def _():
            pltpu.make_async_copy(staged.at[b], pieces.at[ctx], piece_sem.at[1]).start()

        @pl.when(jnp.logical_not(mine))
        def _():
            pltpu.make_async_remote_copy(
                src_ref=staged.at[b],
                dst_ref=pieces.at[ctx],
                send_sem=piece_sem.at[0],
                recv_sem=piece_sem.at[1],
                device_id=(row_group + to_core, to_ctx),
                device_id_type=MESH,
            ).start()

        return 0

    lax.fori_loop(0, 16, send_piece, 0)
    pltpu.make_async_copy(pieces, pieces, piece_sem.at[1]).wait()

    for j in range(16):
        block[6 * j : 6 * j + 6, :] = pieces[j, 0:6, :]
    along_z[x, z, y] = block[0:48, :].astype(jnp.bfloat16)
    along_y[x, y, z] = block[48:96, :].astype(jnp.bfloat16)

    def x_copy(k, which):
        ref = (along_z.at[x, z, y], along_y.at[x, y, z])[which]
        return pltpu.make_async_remote_copy(
            src_ref=ref, dst_ref=ref, send_sem=x_send.at[which, k], recv_sem=x_recv.at[which, k],
            device_id=device(rem(x + k + 1, 4), y, z), device_id_type=MESH,
        )

    for k in range(3):
        x_copy(k, 0).start()
        x_copy(k, 1).start()

    their_tok = pltpu.make_async_remote_copy(
        src_ref=tok_hbm, dst_ref=tok.at[1], send_sem=tok_sem.at[1], recv_sem=tok_sem.at[2],
        device_id=sibling, device_id_type=MESH,
    )
    their_q = pltpu.make_async_remote_copy(
        src_ref=q_hbm.at[:, their_cols], dst_ref=qs.at[1], send_sem=q_sem.at[1],
        recv_sem=q_sem.at[2], device_id=sibling, device_id_type=MESH,
    )
    their_tok.start()
    their_q.start()

    for k in range(3):
        origin = rem(x + 3 - k, 4)
        for which, ref in enumerate((along_z.at[origin, z, y], along_y.at[origin, y, z])):
            pltpu.make_async_copy(ref, ref, x_recv.at[which, k]).wait()

    def first(h):
        upper = along_z.at[h, z, y]
        lower = along_y.at[h, y, z]

        def to_peer(k, _):
            pltpu.make_async_remote_copy(
                src_ref=upper, dst_ref=upper, send_sem=first_send.at[0, h],
                recv_sem=first_recv.at[0, h],
                device_id=device(x, rem(y + k, 8), z), device_id_type=MESH,
            ).start()
            pltpu.make_async_remote_copy(
                src_ref=lower, dst_ref=lower, send_sem=first_send.at[1, h],
                recv_sem=first_recv.at[1, h],
                device_id=device(x, y, rem(z + k, 8)), device_id_type=MESH,
            ).start()
            return 0

        lax.fori_loop(1, 8, to_peer, 0)

    def wait_first(sems, h):
        for axis in range(2):
            ref = along_z.at[h, 0, pl.ds(0, 7)]
            pltpu.make_async_copy(ref, ref, sems.at[axis, h]).wait()

    def part(axis, h, at, which):
        return (along_z, along_y)[axis].at[h, at, (pl.ds(0, 8), pl.ds(0, 4), pl.ds(4, 4))[which]]

    def ring_copy(axis, way, h, step, received, last):
        here = (z, y)[axis]
        sign = 1 - 2 * way
        origin = rem(here - sign * (step + (1 if received else 0)) + 16, 8)
        which = 1 + way if last else 0
        target = rem(here + sign + 8, 8)
        ref = part(axis, h, origin, which)
        return pltpu.make_async_remote_copy(
            src_ref=ref, dst_ref=ref, send_sem=ring_send.at[axis, way, h, step],
            recv_sem=ring_recv.at[axis, way, h, step],
            device_id=device(x, y, target) if axis == 0 else device(x, target, z),
            device_id_type=MESH,
        )

    def ring_start(h, step, last):
        for axis in range(2):
            for way in range(2):
                ring_copy(axis, way, h, step, False, last).start()

    def ring_pass(h, step, last):
        for axis in range(2):
            for way in range(2):
                ring_copy(axis, way, h, step - 1, True, False).wait_recv()
                ring_copy(axis, way, h, step, False, last).start()

    def ring_wait(h, step, last):
        for axis in range(2):
            for way in range(2):
                ring_copy(axis, way, h, step, True, last).wait_recv()

    def project(h):
        total = jnp.zeros((2 * ROWS, 2 * HD), jnp.float32)
        top = jnp.zeros((8, 2 * HD), jnp.float32)
        for c in range(4):
            sides = []
            for kv in range(2):
                strips = []
                for yy in range(4 * (c % 2), 4 * (c % 2) + 4):
                    for zz in (4 * kv + c // 2, 4 * kv + 2 + c // 2):
                        strips += [along_z[h, zz, yy], along_y[h, yy, zz]]
                sides.append(jnp.concatenate(strips, axis=0))
            both = jnp.concatenate(sides, axis=1)
            rows = tok[:, :, 768 * c : 768 * c + 768].reshape(2 * ROWS, 768)
            total = total + jnp.dot(rows, both, preferred_element_type=jnp.float32)
            size = jnp.abs(both.astype(jnp.float32)).reshape(96, 8, 2 * HD)
            top = jnp.maximum(top, jnp.max(size, axis=0))
        top = jnp.broadcast_to(jnp.max(top, axis=0, keepdims=True), (8, 2 * HD))
        peaks[core, h, 0] = top[:, :HD]
        peaks[core, h, 1] = top[:, HD:]
        keys = total[:, :HD]
        turned = pltpu.roll(keys, 64, 1)
        for s in range(2):
            span = slice(ROWS * s, ROWS * s + ROWS)
            rotated = keys[span] * cosine[...] + turned[span] * sine[...]
            keyval[h, s, 0, 512:768, :] = rotated.astype(jnp.bfloat16)
            keyval[h, s, 1, 512:768, :] = total[span, HD:].astype(jnp.bfloat16)

    def slot(h, s, n):
        return keyval.at[h, s, :, pl.ds(256 * n, 256), :]

    def place(xx, up):
        return (dp, rem(z_hi + up, 4) * 4 + xx)

    def send(src, dst, send_sem, recv_sem, to):
        pltpu.make_async_remote_copy(
            src_ref=src, dst_ref=dst, send_sem=send_sem, recv_sem=recv_sem,
            device_id=to, device_id_type=MESH,
        ).start()

    def near(src, h, s, sem, to):
        send(src, slot(h, s, 1), sem, near_recv.at[h, s], to)

    def far(src, h, s, sem, to):
        send(src, slot(h, s, 0), sem, far_recv.at[h, s], to)

    def early(h):
        sem = early_send.at[h]

        @pl.when(x == 3)
        def _():
            send(slot(h, 0, 2), relay.at[h], sem, relay_recv.at[h], place(3, 1))
            send(slot(h, 1, 2), relay.at[h], sem, relay_recv.at[h], place(0, 0))

        @pl.when(x == 2)
        def _():
            far(slot(h, 0, 2), h, 0, sem, place(0, 1))
            send(slot(h, 1, 2), relay.at[h], sem, relay_recv.at[h], place(1, 0))

        @pl.when(x < 3)
        def _():
            for s in range(2):
                near(slot(h, s, 2), h, s, sem, place(x + 1, 0))

        @pl.when(x == 1)
        def _():
            for s in range(2):
                far(slot(h, s, 2), h, s, sem, place(3, 0))

        @pl.when(x == 0)
        def _():
            send(slot(h, 1, 2), detour.at[h], sem, detour_recv.at[h], place(3, 0))

    def wait_slot(sems, h, s, n):
        pltpu.make_async_copy(slot(h, s, n), slot(h, s, n), sems.at[h, s]).wait()

    def late(h):
        sem = late_send.at[h]

        @pl.when(x != 2)
        def _():
            pltpu.make_async_copy(relay.at[h], relay.at[h], relay_recv.at[h]).wait()

        @pl.when(x == 0)
        def _():
            near(relay.at[h], h, 1, sem, place(0, 1))

            @pl.when(h == 3)
            def _():
                far(relay.at[h], h, 1, sem, place(1, 1))

        @pl.when(x == 1)
        def _():
            far(relay.at[h], h, 1, sem, place(0, 1))
            wait_slot(near_recv, h, 0, 1)
            far(slot(h, 0, 1), h, 0, sem, place(2, 0))

        @pl.when(x == 3)
        def _():
            near(relay.at[h], h, 0, sem, place(0, 0))
            far(relay.at[h], h, 0, sem, place(1, 0))
            pltpu.make_async_copy(detour.at[h], detour.at[h], detour_recv.at[h]).wait()
            far(detour.at[h], h, 1, sem, place(2, 0))

    def wait_halo(h):
        wait_slot(near_recv, h, 1, 1)

        @pl.when((x == 0) & (h < 3))
        def _():
            far(slot(h, 1, 1), h, 1, late_send.at[h], place(1, 0))

        @pl.when(x != 1)
        def _():
            wait_slot(near_recv, h, 0, 1)

        for s in range(2):
            wait_slot(far_recv, h, s, 0)

    def wait_sent(sem, n):
        ref = keyval.at[0, :, :, pl.ds(0, 128 * n), :]
        pltpu.make_async_copy(ref, ref, sem).wait()

    def halo_sent(h):
        @pl.when(x == 0)
        def _():
            wait_sent(early_send.at[h], 3)
            wait_sent(late_send.at[h], 2)

        @pl.when(x == 1)
        def _():
            wait_sent(early_send.at[h], 4)
            wait_sent(late_send.at[h], 2)

        @pl.when(x == 2)
        def _():
            wait_sent(early_send.at[h], 4)

        @pl.when(x == 3)
        def _():
            wait_sent(early_send.at[h], 2)
            wait_sent(late_send.at[h], 3)

    row_id = lax.broadcasted_iota(jnp.int32, (2 * 128, 128), 0)
    row_id = jnp.where(row_id >= 128, row_id - 128, row_id)
    col_id = lax.broadcasted_iota(jnp.int32, (2 * 128, 128), 1)
    past = col_id > row_id

    def attend(h):
        def one(i, _):
            s, a = 1 - div(i, 2), rem(i, 2)
            start = pl.multiple_of(a * 128, 128)
            cols = pl.ds(pl.multiple_of(h * 256, 256), 256)
            q = qs[s, pl.ds(start, 128), cols]
            q = jnp.concatenate([q[:, :HD], q[:, HD:]], axis=0)
            keys = keyval[h, s, 0, pl.ds(start, 640), :]
            values = keyval[h, s, 1, pl.ds(start, 640), :]
            scores = lax.dot_general(
                q, keys, (((1,), (1,)), ((), ())), preferred_element_type=jnp.float32
            )
            weight = jnp.exp2(jnp.tanh(scores * (1.0 / 600.0)) * (soft_cap * LOG2E))
            tiles = []
            for t in range(5):
                tile = weight[:, 128 * t : 128 * t + 128]
                inside = (128 * t - 512 + ctx * 256 + start) >= 0
                if t == 0:
                    tile = jnp.where(past & inside, tile, 0.0)
                elif t == 4:
                    tile = jnp.where(past, 0.0, tile)
                else:
                    tile = jnp.where(inside, tile, 0.0)
                tiles.append(tile)
            norm = jnp.sum(tiles[0] + tiles[1] + tiles[2] + tiles[3] + tiles[4], axis=1, keepdims=True)
            weight = jnp.concatenate([t.astype(jnp.bfloat16) for t in tiles], axis=1)
            mixed = jnp.dot(weight, values, preferred_element_type=jnp.float32)
            mixed = (mixed / norm).astype(jnp.bfloat16)
            mixed = jnp.concatenate([mixed[:128], mixed[128:]], axis=1)

            @pl.when(s == 0)
            def _():
                out_cols = pl.ds(pl.multiple_of(core * 1024 + h * 256, 256), 256)
                attended[pl.ds(start, 128), out_cols] = mixed

            @pl.when(s == 1)
            def _():
                sent_out[h, pl.ds(start, 128), :] = mixed

            @pl.when(i == 1)
            def _():
                out_copy(h).start()

            return 0

        lax.fori_loop(0, 4, one, 0)

    def out_copy(h):
        out_cols = pl.ds(pl.multiple_of(core * 1024 + h * 256, 256), 256)
        return pltpu.make_async_remote_copy(
            src_ref=sent_out.at[h], dst_ref=attended.at[:, out_cols],
            send_sem=out_send.at[h], recv_sem=out_recv.at[h],
            device_id=sibling, device_id_type=MESH,
        )


    peak_copy = pltpu.make_async_remote_copy(
        src_ref=peaks.at[core], dst_ref=peaks.at[core], send_sem=peak_sem.at[0],
        recv_sem=peak_sem.at[1], device_id=sibling, device_id_type=MESH,
    )

    def event(e):
        h, kind_of = rem(e, 4), div(e, 4)

        @pl.when(kind_of == START)
        def _():
            first(h)

        @pl.when(kind_of == 0)
        def _():
            wait_first(first_recv, h)

        @pl.when(kind_of == 0)
        def _():
            ring_start(h, 0, False)

        @pl.when((kind_of >= 1) & (kind_of < 3))
        def _():
            ring_pass(h, kind_of, False)

        @pl.when(kind_of == 3)
        def _():
            ring_pass(h, 3, True)

        @pl.when(kind_of == PROJECT)
        def _():
            ring_wait(h, 3, True)

            @pl.when(h == 0)
            def _():
                own_tok.wait()
                their_tok.wait()

            project(h)
            early(h)

            @pl.when(h == 3)
            def _():
                peak_copy.start()

        @pl.when(kind_of == LATE)
        def _():
            late(h)

        @pl.when(kind_of == ATTEND)
        def _():
            wait_halo(h)

            @pl.when(h == 0)
            def _():
                own_q.wait()
                their_q.wait()

            attend(h)

    def group(i, _):
        word = jnp.int32(0)
        for k in range(8):
            coded = 0
            for e in reversed(ORDER[4 * k : 4 * k + 4]):
                coded = coded * 32 + e
            word = jnp.where(i == k, jnp.int32(coded), word)

        def one(_, word):
            event(rem(word, 32))
            return div(word, 32)

        lax.fori_loop(0, 4, one, word)
        return 0

    lax.fori_loop(0, 8, group, 0)


    @pl.when(half == core)
    def _():
        ref = staged.at[pl.ds(0, 15)]
        pltpu.make_async_copy(ref, ref, piece_sem.at[0]).wait()

    @pl.when(half != core)
    def _():
        pltpu.make_async_copy(staged, staged, piece_sem.at[0]).wait()

    for k in range(3):
        x_copy(k, 0).wait_send()
        x_copy(k, 1).wait_send()

    def drain(h, _):
        wait_first(first_send, h)
        for step in range(4):
            for axis in range(2):
                for way in range(2):
                    ring_copy(axis, way, h, step, False, step == 3).wait_send()
        halo_sent(h)
        out_copy(h).wait_send()
        theirs = pl.ds(pl.multiple_of((1 - core) * 1024 + h * 256, 256), 256)
        ref = attended.at[:, theirs]
        pltpu.make_async_copy(ref, ref, out_recv.at[h]).wait()
        return 0

    lax.fori_loop(0, HEADS, drain, 0)

    peak_copy.wait_send()
    ref = peaks.at[1 - core]
    pltpu.make_async_copy(ref, ref, peak_sem.at[1]).wait()
    for b in range(16):
        head = b % 8
        peak_out[:, 128 * b : 128 * b + 128] = peaks[head // 4, head % 4, b // 8, 0:1, :] + 1e-06


def adamw(master, grad, moment, second):
    new_moment = beta_one * moment + (1.0 - beta_one) * grad
    new_second = beta_two * second + (1.0 - beta_two) * grad * grad
    moment_hat = new_moment / (1.0 - beta_one**step_count)
    second_hat = new_second / (1.0 - beta_two**step_count)
    update = moment_hat / (jnp.sqrt(second_hat) + adam_eps) + decay_rate * master
    return (master - learn_rate * update, new_moment, new_second)


def on_device(tokens, queries, master, grad, moment, second):
    new_master, new_moment, new_second = adamw(master, grad, moment, second)
    query_start = lax.axis_index("ctx") * ROWS
    positions = query_start + jnp.arange(ROWS, dtype=jnp.int32)
    freqs = rope_base ** (-jnp.arange(HD // 2, dtype=jnp.float32) * 2.0 / HD)
    angles = positions.astype(jnp.float32)[:, None] * freqs[None, :]
    cosine, sine = jnp.cos(angles), jnp.sin(angles)
    cosine = jnp.concatenate([cosine, cosine], axis=1)
    sine = jnp.concatenate([-sine, sine], axis=1)
    vmem = pl.BlockSpec(memory_space=pltpu.VMEM)
    hbm = pl.BlockSpec(memory_space=pl.ANY)
    dma = pltpu.SemaphoreType.DMA
    f32, bf16 = jnp.float32, jnp.bfloat16
    attended, peak = pl.pallas_call(
        kernel,
        out_shape=(
            jax.ShapeDtypeStruct((ROWS, KVW), bf16),
            jax.ShapeDtypeStruct((1, KVW), f32),
        ),
        in_specs=[hbm] * 2 + [vmem] * 3,
        out_specs=(vmem,) * 2,
        scratch_shapes=[
            pltpu.VMEM((HEADS, 8, 8, 48, HD), bf16),
            pltpu.VMEM((HEADS, 8, 8, 48, HD), bf16),
            pltpu.VMEM((2, ROWS, WIDTH), bf16),
            pltpu.VMEM((2, ROWS, 1024), bf16),
            pltpu.VMEM((HEADS, 2, 2, 768, HD), bf16),
            pltpu.VMEM((HEADS, 2, ROWS, HD), bf16),
            pltpu.VMEM((HEADS, 2, ROWS, HD), bf16),
            pltpu.VMEM((HEADS, ROWS, 256), bf16),
            pltpu.VMEM((16, 8, 128), f32),
            pltpu.VMEM((16, 8, 128), f32),
            pltpu.VMEM((96, 128), f32),
            pltpu.VMEM((2, HEADS, 2, 8, 128), f32),
            dma((3,)),
            dma((3,)),
            dma((2,)),
            dma((2, 3)),
            dma((2, 3)),
            dma((2, HEADS)),
            dma((2, HEADS)),
            dma((2, 2, HEADS, 4)),
            dma((2, 2, HEADS, 4)),
            dma((HEADS,)),
            dma((HEADS,)),
            dma((HEADS, 2)),
            dma((HEADS, 2)),
            dma((HEADS,)),
            dma((HEADS,)),
            dma((HEADS,)),
            dma((HEADS,)),
            dma((2,)),
        ],
        compiler_params=pltpu.CompilerParams(
            collective_id=0, has_side_effects=True, vmem_limit_bytes=LIMIT * 1024 * 1024
        ),
    )(tokens[0], queries[0], new_master, cosine, sine)
    codes = (new_master / peak).astype(bf16)
    return (new_master, new_moment, new_second, codes, attended[None])


def solution(mesh):
    rows = P(("dp", "ctx"), None)
    return jax.shard_map(
        on_device,
        mesh=mesh,
        in_specs=(P("dp", "ctx", None), P("dp", "ctx", None), rows, rows, rows, rows),
        out_specs=(rows, rows, rows, rows, P("dp", "ctx", None)),
        check_vma=False,
    )
```

```python
import jax
import jax.numpy as jnp
from jax import lax
from jax.experimental import pallas as pl
from jax.experimental.pallas import tpu as pltpu
from jax.sharding import PartitionSpec as P

HD = 128
KVH = 8
WINDOW = 512
GROUP = 2
ROWS = 256
WIDTH = 3072
KVW = 2048

beta_one = 0.9
beta_two = 0.95
adam_eps = 1e-08
decay_rate = 0.1
learn_rate = 0.001
step_count = 1000
soft_cap = 50.0
rope_base = 10000.0

MESH = pl.DeviceIdType.MESH
LIMIT = 52
HEADS = 4
LOG2E = 1.4426950408889634


PROJECT, LATE, ATTEND, START = 4, 5, 6, 7


def listed(text):
    kinds = {"0": 0, "1": 1, "2": 2, "3": 3, "P": PROJECT, "L": LATE, "A": ATTEND, "S": START}
    return [4 * kinds[item[0]] + int(item[1]) for item in text.split()]


ORDER = listed('S0 S1 00 S2')
ORDER += listed('01 S3 10 11')
ORDER += listed('20 02 21 30')
ORDER += listed('12 P0 31 03')
ORDER += listed('22 L0 P1 13')
ORDER += listed('32 23 P2 L1')
ORDER += listed('33 A0 P3 L2')
ORDER += listed('A1 L3 A2 A3')


def rem(a, b):
    return lax.rem(a, jnp.int32(b))


def div(a, b):
    return lax.div(a, jnp.int32(b))


def kernel(
    tok_hbm, q_hbm, fresh, cosine, sine,
    attended, peak_out,
    along_z, along_y, tok, qs, keyval, relay, detour, sent_out, staged, pieces, block, peaks,
    tok_sem, q_sem, piece_sem, x_send, x_recv, first_send, first_recv,
    ring_send, ring_recv, early_send, late_send, near_recv, far_recv, relay_recv, detour_recv,
    out_send, out_recv, peak_sem,
):
    dp, ctx = lax.axis_index("dp"), lax.axis_index("ctx")
    core, y, z_lo = rem(dp, 2), rem(div(dp, 2), 8), div(dp, 16)
    x, z_hi = rem(ctx, 4), div(ctx, 4)
    z = 2 * z_hi + z_lo
    kind, half = div(z_hi, 2), rem(z_hi, 2)
    row_group = (z_lo * 8 + y) * 2

    def device(xx, yy, zz):
        return ((rem(zz, 2) * 8 + yy) * 2 + core, div(zz, 2) * 4 + xx)

    sibling = (row_group + 1 - core, ctx)
    barrier = pltpu.get_barrier_semaphore()

    def greet(i, _):
        to_core, to_ctx = rem(i, 2), div(i, 2)

        @pl.when((to_core != core) | (to_ctx != ctx))
        def _():
            pl.semaphore_signal(
                barrier, inc=1, device_id=(row_group + to_core, to_ctx), device_id_type=MESH
            )

        return 0

    lax.fori_loop(0, 32, greet, 0)

    def greet_y(k, _):
        pl.semaphore_signal(
            barrier, inc=1, device_id=device(x, rem(y + k, 8), z), device_id_type=MESH
        )
        return 0

    lax.fori_loop(1, 8, greet_y, 0)

    def greet_z(k, _):
        pl.semaphore_signal(
            barrier, inc=1, device_id=device(x, y, rem(z + 2 * k + 1, 8)), device_id_type=MESH
        )
        return 0

    lax.fori_loop(0, 4, greet_z, 0)

    own_cols = pl.ds(pl.multiple_of(core * 1024, 1024), 1024)
    their_cols = pl.ds(pl.multiple_of((1 - core) * 1024, 1024), 1024)
    own_tok = pltpu.make_async_copy(tok_hbm, tok.at[0], tok_sem.at[0])
    own_q = pltpu.make_async_copy(q_hbm.at[:, own_cols], qs.at[0], q_sem.at[0])
    own_tok.start()
    own_q.start()

    staged[...] = jnp.zeros_like(staged)
    for b in range(16):
        staged[b, 0:6, :] = fresh[:, 128 * b : 128 * b + 128]

    pl.semaphore_wait(barrier, 42)

    def owner(b):
        head = rem(b, 8)
        return div(head, 4), (div(b, 8) * 2 + core) * 4 + rem(head, 4)

    def send_piece(b, _):
        to_core, to_ctx = owner(b)
        mine = (to_core == core) & (to_ctx == ctx)

        @pl.when(mine)
        def _():
            pltpu.make_async_copy(staged.at[b], pieces.at[ctx], piece_sem.at[1]).start()

        @pl.when(jnp.logical_not(mine))
        def _():
            pltpu.make_async_remote_copy(
                src_ref=staged.at[b],
                dst_ref=pieces.at[ctx],
                send_sem=piece_sem.at[0],
                recv_sem=piece_sem.at[1],
                device_id=(row_group + to_core, to_ctx),
                device_id_type=MESH,
            ).start()

        return 0

    lax.fori_loop(0, 16, send_piece, 0)
    pltpu.make_async_copy(pieces, pieces, piece_sem.at[1]).wait()

    for j in range(16):
        block[6 * j : 6 * j + 6, :] = pieces[j, 0:6, :]
    along_z[x, z, y] = block[0:48, :].astype(jnp.bfloat16)
    along_y[x, y, z] = block[48:96, :].astype(jnp.bfloat16)

    def x_copy(k, which):
        ref = (along_z.at[x, z, y], along_y.at[x, y, z])[which]
        return pltpu.make_async_remote_copy(
            src_ref=ref, dst_ref=ref, send_sem=x_send.at[which, k], recv_sem=x_recv.at[which, k],
            device_id=device(rem(x + k + 1, 4), y, z), device_id_type=MESH,
        )

    for k in range(3):
        x_copy(k, 0).start()
        x_copy(k, 1).start()

    their_tok = pltpu.make_async_remote_copy(
        src_ref=tok_hbm, dst_ref=tok.at[1], send_sem=tok_sem.at[1], recv_sem=tok_sem.at[2],
        device_id=sibling, device_id_type=MESH,
    )
    their_q = pltpu.make_async_remote_copy(
        src_ref=q_hbm.at[:, their_cols], dst_ref=qs.at[1], send_sem=q_sem.at[1],
        recv_sem=q_sem.at[2], device_id=sibling, device_id_type=MESH,
    )
    their_tok.start()
    their_q.start()

    for k in range(3):
        origin = rem(x + 3 - k, 4)
        for which, ref in enumerate((along_z.at[origin, z, y], along_y.at[origin, y, z])):
            pltpu.make_async_copy(ref, ref, x_recv.at[which, k]).wait()

    def first(h):
        upper = along_z.at[h, z, y]
        lower = along_y.at[h, y, z]

        def to_peer(k, _):
            pltpu.make_async_remote_copy(
                src_ref=upper, dst_ref=upper, send_sem=first_send.at[0, h],
                recv_sem=first_recv.at[0, h],
                device_id=device(x, rem(y + k, 8), z), device_id_type=MESH,
            ).start()
            pltpu.make_async_remote_copy(
                src_ref=lower, dst_ref=lower, send_sem=first_send.at[1, h],
                recv_sem=first_recv.at[1, h],
                device_id=device(x, y, rem(z + k, 8)), device_id_type=MESH,
            ).start()
            return 0

        lax.fori_loop(1, 8, to_peer, 0)

    def wait_first(sems, h):
        for axis in range(2):
            ref = along_z.at[h, 0, pl.ds(0, 7)]
            pltpu.make_async_copy(ref, ref, sems.at[axis, h]).wait()

    def part(axis, h, at, which):
        return (along_z, along_y)[axis].at[h, at, (pl.ds(0, 8), pl.ds(0, 4), pl.ds(4, 4))[which]]

    def ring_copy(axis, way, h, step, received, last):
        here = (z, y)[axis]
        sign = 1 - 2 * way
        origin = rem(here - sign * (step + (1 if received else 0)) + 16, 8)
        which = 1 + way if last else 0
        target = rem(here + sign + 8, 8)
        ref = part(axis, h, origin, which)
        return pltpu.make_async_remote_copy(
            src_ref=ref, dst_ref=ref, send_sem=ring_send.at[axis, way, h, step],
            recv_sem=ring_recv.at[axis, way, h, step],
            device_id=device(x, y, target) if axis == 0 else device(x, target, z),
            device_id_type=MESH,
        )

    def ring_start(h, step, last):
        for axis in range(2):
            for way in range(2):
                ring_copy(axis, way, h, step, False, last).start()

    def ring_pass(h, step, last):
        for axis in range(2):
            for way in range(2):
                ring_copy(axis, way, h, step - 1, True, False).wait_recv()
                ring_copy(axis, way, h, step, False, last).start()

    def ring_wait(h, step, last):
        for axis in range(2):
            for way in range(2):
                ring_copy(axis, way, h, step, True, last).wait_recv()

    def project(h):
        total = jnp.zeros((2 * ROWS, 2 * HD), jnp.float32)
        top = jnp.zeros((8, 2 * HD), jnp.float32)
        for c in range(4):
            sides = []
            for kv in range(2):
                strips = []
                for yy in range(4 * (c % 2), 4 * (c % 2) + 4):
                    for zz in (4 * kv + c // 2, 4 * kv + 2 + c // 2):
                        strips += [along_z[h, zz, yy], along_y[h, yy, zz]]
                sides.append(jnp.concatenate(strips, axis=0))
            both = jnp.concatenate(sides, axis=1)
            rows = tok[:, :, 768 * c : 768 * c + 768].reshape(2 * ROWS, 768)
            total = total + jnp.dot(rows, both, preferred_element_type=jnp.float32)
            size = jnp.abs(both.astype(jnp.float32)).reshape(96, 8, 2 * HD)
            top = jnp.maximum(top, jnp.max(size, axis=0))
        top = jnp.broadcast_to(jnp.max(top, axis=0, keepdims=True), (8, 2 * HD))
        peaks[core, h, 0] = top[:, :HD]
        peaks[core, h, 1] = top[:, HD:]
        keys = total[:, :HD]
        turned = pltpu.roll(keys, 64, 1)
        for s in range(2):
            span = slice(ROWS * s, ROWS * s + ROWS)
            rotated = keys[span] * cosine[...] + turned[span] * sine[...]
            keyval[h, s, 0, 512:768, :] = rotated.astype(jnp.bfloat16)
            keyval[h, s, 1, 512:768, :] = total[span, HD:].astype(jnp.bfloat16)

    def slot(h, s, n):
        return keyval.at[h, s, :, pl.ds(256 * n, 256), :]

    def place(xx, up):
        return (dp, rem(z_hi + up, 4) * 4 + xx)

    def send(src, dst, send_sem, recv_sem, to):
        pltpu.make_async_remote_copy(
            src_ref=src, dst_ref=dst, send_sem=send_sem, recv_sem=recv_sem,
            device_id=to, device_id_type=MESH,
        ).start()

    def near(src, h, s, sem, to):
        send(src, slot(h, s, 1), sem, near_recv.at[h, s], to)

    def far(src, h, s, sem, to):
        send(src, slot(h, s, 0), sem, far_recv.at[h, s], to)

    def early(h):
        sem = early_send.at[h]

        @pl.when(x == 3)
        def _():
            send(slot(h, 0, 2), relay.at[h], sem, relay_recv.at[h], place(3, 1))
            send(slot(h, 1, 2), relay.at[h], sem, relay_recv.at[h], place(0, 0))

        @pl.when(x == 2)
        def _():
            far(slot(h, 0, 2), h, 0, sem, place(0, 1))
            send(slot(h, 1, 2), relay.at[h], sem, relay_recv.at[h], place(1, 0))

        @pl.when(x < 3)
        def _():
            for s in range(2):
                near(slot(h, s, 2), h, s, sem, place(x + 1, 0))

        @pl.when(x == 1)
        def _():
            for s in range(2):
                far(slot(h, s, 2), h, s, sem, place(3, 0))

        @pl.when(x == 0)
        def _():
            send(slot(h, 1, 2), detour.at[h], sem, detour_recv.at[h], place(3, 0))

    def wait_slot(sems, h, s, n):
        pltpu.make_async_copy(slot(h, s, n), slot(h, s, n), sems.at[h, s]).wait()

    def late(h):
        sem = late_send.at[h]

        @pl.when(x != 2)
        def _():
            pltpu.make_async_copy(relay.at[h], relay.at[h], relay_recv.at[h]).wait()

        @pl.when(x == 0)
        def _():
            near(relay.at[h], h, 1, sem, place(0, 1))

            @pl.when(h == 3)
            def _():
                far(relay.at[h], h, 1, sem, place(1, 1))

        @pl.when(x == 1)
        def _():
            far(relay.at[h], h, 1, sem, place(0, 1))
            wait_slot(near_recv, h, 0, 1)
            far(slot(h, 0, 1), h, 0, sem, place(2, 0))

        @pl.when(x == 3)
        def _():
            near(relay.at[h], h, 0, sem, place(0, 0))
            far(relay.at[h], h, 0, sem, place(1, 0))
            pltpu.make_async_copy(detour.at[h], detour.at[h], detour_recv.at[h]).wait()
            far(detour.at[h], h, 1, sem, place(2, 0))

    def wait_halo(h):
        wait_slot(near_recv, h, 1, 1)

        @pl.when((x == 0) & (h < 3))
        def _():
            far(slot(h, 1, 1), h, 1, late_send.at[h], place(1, 0))

        @pl.when(x != 1)
        def _():
            wait_slot(near_recv, h, 0, 1)

        for s in range(2):
            wait_slot(far_recv, h, s, 0)

    def wait_sent(sem, n):
        ref = keyval.at[0, :, :, pl.ds(0, 128 * n), :]
        pltpu.make_async_copy(ref, ref, sem).wait()

    def halo_sent(h):
        @pl.when(x == 0)
        def _():
            wait_sent(early_send.at[h], 3)
            wait_sent(late_send.at[h], 2)

        @pl.when(x == 1)
        def _():
            wait_sent(early_send.at[h], 4)
            wait_sent(late_send.at[h], 2)

        @pl.when(x == 2)
        def _():
            wait_sent(early_send.at[h], 4)

        @pl.when(x == 3)
        def _():
            wait_sent(early_send.at[h], 2)
            wait_sent(late_send.at[h], 3)

    row_id = lax.broadcasted_iota(jnp.int32, (2 * 128, 128), 0)
    row_id = jnp.where(row_id >= 128, row_id - 128, row_id)
    col_id = lax.broadcasted_iota(jnp.int32, (2 * 128, 128), 1)
    past = col_id > row_id

    def attend(h):
        def one(i, _):
            s, a = 1 - div(i, 2), rem(i, 2)
            start = pl.multiple_of(a * 128, 128)
            cols = pl.ds(pl.multiple_of(h * 256, 256), 256)
            q = qs[s, pl.ds(start, 128), cols]
            q = jnp.concatenate([q[:, :HD], q[:, HD:]], axis=0)
            keys = keyval[h, s, 0, pl.ds(start, 640), :]
            values = keyval[h, s, 1, pl.ds(start, 640), :]
            scores = lax.dot_general(
                q, keys, (((1,), (1,)), ((), ())), preferred_element_type=jnp.float32
            )
            weight = jnp.exp2(jnp.tanh(scores * (1.0 / 600.0)) * (soft_cap * LOG2E))
            tiles = []
            for t in range(5):
                tile = weight[:, 128 * t : 128 * t + 128]
                inside = (128 * t - 512 + ctx * 256 + start) >= 0
                if t == 0:
                    tile = jnp.where(past & inside, tile, 0.0)
                elif t == 4:
                    tile = jnp.where(past, 0.0, tile)
                else:
                    tile = jnp.where(inside, tile, 0.0)
                tiles.append(tile)
            norm = jnp.sum(tiles[0] + tiles[1] + tiles[2] + tiles[3] + tiles[4], axis=1, keepdims=True)
            weight = jnp.concatenate([t.astype(jnp.bfloat16) for t in tiles], axis=1)
            mixed = jnp.dot(weight, values, preferred_element_type=jnp.float32)
            mixed = (mixed / norm).astype(jnp.bfloat16)
            mixed = jnp.concatenate([mixed[:128], mixed[128:]], axis=1)

            @pl.when(s == 0)
            def _():
                out_cols = pl.ds(pl.multiple_of(core * 1024 + h * 256, 256), 256)
                attended[pl.ds(start, 128), out_cols] = mixed

            @pl.when(s == 1)
            def _():
                sent_out[h, pl.ds(start, 128), :] = mixed

            @pl.when(i == 1)
            def _():
                out_copy(h).start()

            return 0

        lax.fori_loop(0, 4, one, 0)

    def out_copy(h):
        out_cols = pl.ds(pl.multiple_of(core * 1024 + h * 256, 256), 256)
        return pltpu.make_async_remote_copy(
            src_ref=sent_out.at[h], dst_ref=attended.at[:, out_cols],
            send_sem=out_send.at[h], recv_sem=out_recv.at[h],
            device_id=sibling, device_id_type=MESH,
        )


    peak_copy = pltpu.make_async_remote_copy(
        src_ref=peaks.at[core], dst_ref=peaks.at[core], send_sem=peak_sem.at[0],
        recv_sem=peak_sem.at[1], device_id=sibling, device_id_type=MESH,
    )

    def event(e):
        h, kind_of = rem(e, 4), div(e, 4)

        @pl.when(kind_of == START)
        def _():
            first(h)

        @pl.when(kind_of == 0)
        def _():
            wait_first(first_recv, h)

        @pl.when(kind_of == 0)
        def _():
            ring_start(h, 0, False)

        @pl.when((kind_of >= 1) & (kind_of < 3))
        def _():
            ring_pass(h, kind_of, False)

        @pl.when(kind_of == 3)
        def _():
            ring_pass(h, 3, True)

        @pl.when(kind_of == PROJECT)
        def _():
            ring_wait(h, 3, True)

            @pl.when(h == 0)
            def _():
                own_tok.wait()
                their_tok.wait()

            project(h)
            early(h)

            @pl.when(h == 3)
            def _():
                peak_copy.start()

        @pl.when(kind_of == LATE)
        def _():
            late(h)

        @pl.when(kind_of == ATTEND)
        def _():
            wait_halo(h)

            @pl.when(h == 0)
            def _():
                own_q.wait()
                their_q.wait()

            attend(h)

    def group(i, _):
        word = jnp.int32(0)
        for k in range(8):
            coded = 0
            for e in reversed(ORDER[4 * k : 4 * k + 4]):
                coded = coded * 32 + e
            word = jnp.where(i == k, jnp.int32(coded), word)

        def one(_, word):
            event(rem(word, 32))
            return div(word, 32)

        lax.fori_loop(0, 4, one, word)
        return 0

    lax.fori_loop(0, 8, group, 0)


    @pl.when(half == core)
    def _():
        ref = staged.at[pl.ds(0, 15)]
        pltpu.make_async_copy(ref, ref, piece_sem.at[0]).wait()

    @pl.when(half != core)
    def _():
        pltpu.make_async_copy(staged, staged, piece_sem.at[0]).wait()

    for k in range(3):
        x_copy(k, 0).wait_send()
        x_copy(k, 1).wait_send()

    def drain(h, _):
        wait_first(first_send, h)
        for step in range(4):
            for axis in range(2):
                for way in range(2):
                    ring_copy(axis, way, h, step, False, step == 3).wait_send()
        halo_sent(h)
        out_copy(h).wait_send()
        theirs = pl.ds(pl.multiple_of((1 - core) * 1024 + h * 256, 256), 256)
        ref = attended.at[:, theirs]
        pltpu.make_async_copy(ref, ref, out_recv.at[h]).wait()
        return 0

    lax.fori_loop(0, HEADS, drain, 0)

    peak_copy.wait_send()
    ref = peaks.at[1 - core]
    pltpu.make_async_copy(ref, ref, peak_sem.at[1]).wait()
    for b in range(16):
        head = b % 8
        peak_out[:, 128 * b : 128 * b + 128] = peaks[head // 4, head % 4, b // 8, 0:1, :] + 1e-06


def adamw(master, grad, moment, second):
    new_moment = beta_one * moment + (1.0 - beta_one) * grad
    new_second = beta_two * second + (1.0 - beta_two) * grad * grad
    moment_hat = new_moment / (1.0 - beta_one**step_count)
    second_hat = new_second / (1.0 - beta_two**step_count)
    update = moment_hat / (jnp.sqrt(second_hat) + adam_eps) + decay_rate * master
    return (master - learn_rate * update, new_moment, new_second)


def on_device(tokens, queries, master, grad, moment, second):
    new_master, new_moment, new_second = adamw(master, grad, moment, second)
    query_start = lax.axis_index("ctx") * ROWS
    positions = query_start + jnp.arange(ROWS, dtype=jnp.int32)
    freqs = rope_base ** (-jnp.arange(HD // 2, dtype=jnp.float32) * 2.0 / HD)
    angles = positions.astype(jnp.float32)[:, None] * freqs[None, :]
    cosine, sine = jnp.cos(angles), jnp.sin(angles)
    cosine = jnp.concatenate([cosine, cosine], axis=1)
    sine = jnp.concatenate([-sine, sine], axis=1)
    vmem = pl.BlockSpec(memory_space=pltpu.VMEM)
    hbm = pl.BlockSpec(memory_space=pl.ANY)
    dma = pltpu.SemaphoreType.DMA
    f32, bf16 = jnp.float32, jnp.bfloat16
    attended, peak = pl.pallas_call(
        kernel,
        out_shape=(
            jax.ShapeDtypeStruct((ROWS, KVW), bf16),
            jax.ShapeDtypeStruct((1, KVW), f32),
        ),
        in_specs=[hbm] * 2 + [vmem] * 3,
        out_specs=(vmem,) * 2,
        scratch_shapes=[
            pltpu.VMEM((HEADS, 8, 8, 48, HD), bf16),
            pltpu.VMEM((HEADS, 8, 8, 48, HD), bf16),
            pltpu.VMEM((2, ROWS, WIDTH), bf16),
            pltpu.VMEM((2, ROWS, 1024), bf16),
            pltpu.VMEM((HEADS, 2, 2, 768, HD), bf16),
            pltpu.VMEM((HEADS, 2, ROWS, HD), bf16),
            pltpu.VMEM((HEADS, 2, ROWS, HD), bf16),
            pltpu.VMEM((HEADS, ROWS, 256), bf16),
            pltpu.VMEM((16, 8, 128), f32),
            pltpu.VMEM((16, 8, 128), f32),
            pltpu.VMEM((96, 128), f32),
            pltpu.VMEM((2, HEADS, 2, 8, 128), f32),
            dma((3,)),
            dma((3,)),
            dma((2,)),
            dma((2, 3)),
            dma((2, 3)),
            dma((2, HEADS)),
            dma((2, HEADS)),
            dma((2, 2, HEADS, 4)),
            dma((2, 2, HEADS, 4)),
            dma((HEADS,)),
            dma((HEADS,)),
            dma((HEADS, 2)),
            dma((HEADS, 2)),
            dma((HEADS,)),
            dma((HEADS,)),
            dma((HEADS,)),
            dma((HEADS,)),
            dma((2,)),
        ],
        compiler_params=pltpu.CompilerParams(
            collective_id=0, has_side_effects=True, vmem_limit_bytes=LIMIT * 1024 * 1024
        ),
    )(tokens[0], queries[0], new_master, cosine, sine)
    codes = (new_master / peak).astype(bf16)
    return (new_master, new_moment, new_second, codes, attended[None])


def solution(mesh):
    rows = P(("dp", "ctx"), None)
    return jax.shard_map(
        on_device,
        mesh=mesh,
        in_specs=(P("dp", "ctx", None), P("dp", "ctx", None), rows, rows, rows, rows),
        out_specs=(rows, rows, rows, rows, P("dp", "ctx", None)),
        check_vma=False,
    )
```
